32 devices in a mesh: dp: 4 (over z), pipe: 4 (over x, core), mp: 2 (over y).
Axes of the slice: x: 2, y: 2, z: 4, core: 2. Of those that a mesh axis runs over, the one named last changes fastest.
Arguments:
- latents: bfloat16 [4, 2, 64, 3072], P('dp'), may hold values from -6 to 6
- caption_kv: bfloat16 [4, 4, 2, 128, 1536], P('dp', 'pipe', None, None, 'mp'), may hold values from -6 to 6
- caption_mask: int32 [4, 128], P('dp'), may hold values from 0 to 1, as said below
- query_weight: bfloat16 [4, 3072, 1536], P('pipe', None, 'mp'), may hold values from -0.109375 to 0.109375
- out_weight: bfloat16 [4, 1536, 3072], P('pipe', 'mp'), may hold values from -0.15625 to 0.15625
- gate: float32 [4, 3072], P('pipe'), may hold values from 0.5 to 1.5
- cotangent: bfloat16 [4, 2, 64, 3072], P('dp'), may hold values from -6 to 6
Outputs:
- section_out: bfloat16 [4, 4, 2, 64, 3072], P('pipe', 'dp', None, None, 'mp')
- input_grad: bfloat16 [4, 4, 2, 64, 3072], P('pipe', 'dp', None, None, 'mp')
- out_weight_grad: float32 [4, 1536, 3072], P('pipe', 'mp', 'dp')
The draws below stay inside these ranges and needn't reach their ends.
Inputs may be any that keep to these rules, and one draw needn't show every extreme that they name: `caption_mask`: each row is a run of ones followed by zeros; the first 32 entries of every row are 1, and some row is all ones.
All inputs are finite; a program needn't handle non-finite values.
Results may differ from the reference program's by a relative error of at most 0.04.
Values may be sent and summed in bfloat16 or wider, within the bound.
A program may use at most 64 MiB of HBM per device.

```python
import math
from functools import partial
import jax
import jax.numpy as jnp
from jax import lax

D = 3072
HEADS = 12
HEAD_DIM = 128
CAP = 128
TOK = 64
MICRO = 2
N_DP = 4
N_PIPE = 4


def draw_caption_mask(key, part):
    lengths = jax.random.randint(key, (N_DP,), CAP // 4, CAP + 1)
    lengths = lengths.at[0].set(CAP)
    positions = jnp.arange(CAP, dtype=jnp.int32)
    return (positions[None, :] < lengths[:, None]).astype(jnp.int32)


def with_spikes(drawn, key, source, target, parts, factor):
    owner, partner = [(jnp.arange(drawn.shape[dim]) // (drawn.shape[dim] // parts)).reshape([-1 if axis == dim else 1 for axis in range(drawn.ndim)]) for dim in (source, target)]
    chosen = jax.random.permutation(key, parts)[partner]
    strong = (owner == chosen) | (owner == (partner + parts // 2) % parts)
    return jnp.where(strong, factor * drawn, drawn)


def block_levels(own_key, shape, pieces, smallest, high):
    level = 1.0
    for dim, parts in pieces:
        draws = jax.random.uniform(jax.random.fold_in(jax.random.fold_in(own_key, 6), dim), (parts,), jnp.float32, smallest / len(pieces), high / len(pieces))
        level = level * jnp.repeat(jnp.exp(draws), shape[dim] // parts).reshape((-1,) + (1,) * (len(shape) - 1 - dim))
    return level


def bell_draw(stream_key, extent, deviation, reach, cuts=(), held_as=jnp.bfloat16):
    array = jax.random.normal(stream_key, extent, jnp.float32) * deviation
    if len(cuts) > 0:
        array = block_levels(stream_key, extent, cuts, -0.22, 0.18) * array
    return jnp.clip(array, min=-reach, max=reach).astype(held_as)


def bell_draw_with(rng, extent, spread, bound, cuts, heavy, kind=jnp.bfloat16):
    array = spread * jax.random.normal(rng, extent, jnp.float32)
    if cuts:
        array = array * block_levels(rng, extent, cuts, -0.22, 0.18)
    return jnp.clip(with_spikes(array, jax.random.fold_in(rng, 3), *heavy), -bound, bound).astype(kind)


def setup_inputs(seed: int = 0) -> dict:
    splits = jax.random.split(jax.random.key(seed), 8)
    return {
        "latents": bell_draw(splits[0], (N_DP, MICRO, TOK, D), 1.0, 6.0, ((0, 4),)),
        "caption_kv": bell_draw(splits[1], (N_DP, N_PIPE, 2, CAP, HEADS * HEAD_DIM), 1.0, 6.0, ((0, 4), (1, 4), (4, 2))),
        "caption_mask": draw_caption_mask(jax.random.fold_in(splits[7], 71), 0),
        "query_weight": bell_draw(splits[3], (N_PIPE, D, HEADS * HEAD_DIM), D ** -0.5, 0.109375, ((0, 4), (2, 2))),
        "out_weight": bell_draw(splits[4], (N_PIPE, HEADS * HEAD_DIM, D), (HEADS * HEAD_DIM) ** -0.5, 0.15625, ((0, 4), (1, 2))),
        "gate": jnp.clip(0.5 + 1.0 * jax.random.uniform(splits[5], (N_PIPE, D), jnp.float32) ** block_levels(splits[5], (N_PIPE, D), ((0, 4),), -0.2, 0.2), 0.5, 1.5),
        "cotangent": bell_draw_with(splits[6], (N_DP, MICRO, TOK, D), 1.0, 6.0, ((0, 4),), (0, 3, 4, 2.0)),
    }


def forward_parts(x_rows, w_query, kv_pair, live):
    rows = x_rows.shape[0]
    x_float = x_rows.astype(jnp.float32)
    scale_r = lax.rsqrt(lax.optimization_barrier(jnp.mean(x_float * x_float, axis=-1, keepdims=True)) + 1e-06)
    normed = (x_float * scale_r).astype(jnp.bfloat16)
    query = jnp.dot(normed, w_query, preferred_element_type=jnp.float32).astype(jnp.bfloat16)
    q_heads = query.reshape(rows, -1, HEAD_DIM).astype(jnp.float32)
    k_heads = kv_pair[0].reshape(kv_pair.shape[1], -1, HEAD_DIM).astype(jnp.float32)
    v_heads = kv_pair[1].reshape(kv_pair.shape[1], -1, HEAD_DIM).astype(jnp.float32)
    scores = jnp.einsum('rhd,chd->hrc', q_heads, k_heads) / math.sqrt(HEAD_DIM)
    scores = jnp.where(live[None, None, :] > 0, scores, -1e+30)
    prob = jax.nn.softmax(scores, axis=-1)
    probs = lax.optimization_barrier(prob.astype(jnp.bfloat16)).astype(jnp.float32)
    attended = jnp.einsum('hrc,chd->rhd', probs, v_heads).reshape(rows, -1).astype(jnp.bfloat16)
    return (x_float, scale_r, prob, attended, k_heads, v_heads)

def section_forward(x_rows, w_query, w_out, kv_pair, live, gain):
    x_float, scale_r, prob, attended, k_heads, v_heads = forward_parts(x_rows, w_query, kv_pair, live)
    proj = jnp.dot(attended, w_out, preferred_element_type=jnp.float32)
    return (x_float + gain * proj).astype(jnp.bfloat16)

def section_backward(x_rows, grad_rows, w_query, w_out, kv_pair, live, gain):
    rows = x_rows.shape[0]
    x_float, scale_r, prob, attended, k_heads, v_heads = forward_parts(x_rows, w_query, kv_pair, live)
    grad_float = grad_rows.astype(jnp.float32)
    dproj = (gain * grad_float).astype(jnp.bfloat16)
    dattended = jnp.dot(dproj, w_out.T, preferred_element_type=jnp.float32).astype(jnp.bfloat16)
    d_heads = dattended.reshape(rows, -1, HEAD_DIM).astype(jnp.float32)
    dprob = jnp.einsum('rhd,chd->hrc', d_heads, v_heads)
    dscore = (prob * (dprob - lax.optimization_barrier(jnp.sum(prob * dprob, axis=-1, keepdims=True)))).astype(jnp.bfloat16)
    dscore_f = lax.optimization_barrier(dscore).astype(jnp.float32)
    dquery = (jnp.einsum('hrc,chd->rhd', dscore_f, k_heads) / math.sqrt(HEAD_DIM)).reshape(rows, -1).astype(jnp.bfloat16)
    dnormed = jnp.dot(dquery, w_query.T, preferred_element_type=jnp.float32)
    inner = lax.optimization_barrier(jnp.mean(dnormed * x_float, axis=-1, keepdims=True))
    dx = (grad_float + scale_r * (dnormed - x_float * (scale_r * scale_r) * inner)).astype(jnp.bfloat16)
    return (dx, attended, dproj)

def reference(latents, caption_kv, caption_mask, query_weight, out_weight, gate, cotangent):
    samples, micro, tok, width = latents.shape
    current = latents.reshape(samples, micro * tok, width)
    inputs = []
    outputs = []
    for section in range(N_PIPE):
        step_fn = jax.vmap(partial(section_forward, w_query=query_weight[section], w_out=out_weight[section], gain=gate[section]))
        result = step_fn(current, kv_pair=caption_kv[:, section], live=caption_mask)
        inputs.append(current)
        outputs.append(result)
        current = result
    upstream = cotangent.reshape(samples, micro * tok, width)
    grads = [None] * N_PIPE
    weight_grads = [None] * N_PIPE
    for section in range(N_PIPE - 1, -1, -1):
        back_fn = jax.vmap(partial(section_backward, w_query=query_weight[section], w_out=out_weight[section], gain=gate[section]))
        dx, attended, dproj = back_fn(inputs[section], upstream, kv_pair=caption_kv[:, section], live=caption_mask)
        weight_grads[section] = jnp.einsum('srk,srd->kd', attended.astype(jnp.float32), dproj.astype(jnp.float32))
        grads[section] = dx
        upstream = dx
    section_out = jnp.stack(outputs).reshape(N_PIPE, samples, micro, tok, width)
    input_grad = jnp.stack(grads).reshape(N_PIPE, samples, micro, tok, width)
    return (section_out, input_grad, jnp.stack(weight_grads))
```

```python
import functools
import math

import jax
import jax.numpy as jnp
from jax import lax
from jax.experimental import pallas as pl
from jax.experimental.pallas import tpu as pltpu
from jax.sharding import PartitionSpec as P

HEAD_DIM = 128
GROUPS = 2
CHUNKS = 2
MESH = pl.DeviceIdType.MESH
NT = (((1,), (1,)), ((), ()))
TN = (((0,), (0,)), ((), ()))


def dot(a, b, dims=(((1,), (0,)), ((), ()))):
    return lax.dot_general(a, b, dims, preferred_element_type=jnp.float32)


def relay_kernel(
    sizes,
    lat,
    kv,
    mask,
    wq,
    wo,
    gate,
    cot,
    out_ref,
    dx_ref,
    wg_ref,
    xbuf,
    dybuf,
    xsend,
    dxsend,
    psend,
    precv,
    bsend,
    brecv,
    own,
    prob_buf,
    qbuf,
    rbuf,
    att_all,
    dpj,
    dcol,
    s_x,
    r_x,
    s_dy,
    r_dy,
    s_p,
    r_p,
    s_b,
    r_b,
    s_att,
    r_att,
    s_dp,
    r_dp,
):
    n_dp, n_pipe, n_mp = sizes
    groups, rows, width = lat.shape
    chunks, chunk = (xbuf.shape[2], xbuf.shape[4])
    inner_width = wo.shape[0]
    heads = inner_width // HEAD_DIM
    share = dpj.shape[2]
    slabs = chunk // share
    scale = 1.0 / math.sqrt(HEAD_DIM)
    z = lax.axis_index("dp")
    p = lax.axis_index("pipe")
    y = lax.axis_index("mp")
    first = p == 0
    last = p == n_pipe - 1

    barrier = pltpu.get_barrier_semaphore()

    def greet(target):
        pl.semaphore_signal(barrier, inc=1, device_id=target, device_id_type=MESH)

    for o in range(1, n_mp):
        greet({"mp": lax.rem(y + o, n_mp)})

    @pl.loop(1, n_dp)
    def _(k):
        greet({"dp": lax.rem(z + k, n_dp)})

    @pl.when(jnp.logical_not(first))
    def _():
        for h in range(n_mp):
            greet({"pipe": p - 1, "mp": h})

    @pl.when(jnp.logical_not(last))
    def _():
        for h in range(n_mp):
            greet({"pipe": p + 1, "mp": h})

    @pl.when(first)
    def _():
        for m in range(groups):
            for h in range(n_mp):
                for c in range(chunks):
                    begin = (h * chunks + c) * chunk
                    xbuf[m, h, c] = lat[m, :, begin : begin + chunk]

    @pl.when(last)
    def _():
        for m in range(groups):
            for h in range(n_mp):
                for c in range(chunks):
                    begin = (h * chunks + c) * chunk
                    dybuf[m, h, c] = cot[m, :, begin : begin + chunk]

    edges = first.astype(jnp.int32) + last.astype(jnp.int32)
    pl.semaphore_wait(barrier, (n_mp - 1) + (n_dp - 1) + n_mp * (2 - edges))

    def group_rows(m):
        return pl.ds(pl.multiple_of(m * rows, rows), rows)

    def columns(j):
        return pl.ds(pl.multiple_of(j * chunk, 128), chunk)

    def relay_copy(src, dst, send, recv, m, c, h, target, slot):
        return pltpu.make_async_remote_copy(
            src_ref=src.at[m, c],
            dst_ref=dst.at[m, h, c],
            send_sem=send.at[m, c, slot],
            recv_sem=recv.at[m, h, c],
            device_id=target,
            device_id_type=MESH,
        )

    def forward_copy(m, c, o):
        target = {"pipe": p + 1, "mp": lax.rem(y + o, n_mp)}
        return relay_copy(xsend, xbuf, s_x, r_x, m, c, y, target, o)

    def backward_copy(m, c, o):
        target = {"pipe": p - 1, "mp": lax.rem(y + o, n_mp)}
        return relay_copy(dxsend, dybuf, s_dy, r_dy, m, c, y, target, o)

    def share_copy(src, dst, send, recv, m, c, o):
        return pltpu.make_async_remote_copy(
            src_ref=src.at[m, o - 1, c],
            dst_ref=dst.at[m, o - 1, c],
            send_sem=send.at[m, o - 1, c],
            recv_sem=recv.at[m, o - 1, c],
            device_id={"mp": lax.rem(y + o, n_mp)},
            device_id_type=MESH,
        )

    def att_copy(m, k, source):
        piece = att_all.at[source, group_rows(m)]
        return pltpu.make_async_remote_copy(
            src_ref=piece,
            dst_ref=piece,
            send_sem=s_att.at[m, k],
            recv_sem=r_att.at[m, k],
            device_id={"dp": lax.rem(z + k, n_dp)},
            device_id_type=MESH,
        )

    def dproj_copy(m, k, source, owner):
        return pltpu.make_async_remote_copy(
            src_ref=dpj.at[owner, group_rows(m)],
            dst_ref=dcol.at[source, group_rows(m)],
            send_sem=s_dp.at[m, k],
            recv_sem=r_dp.at[m, k],
            device_id={"dp": lax.rem(z + k, n_dp)},
            device_id_type=MESH,
        )

    def head(t):
        return slice(t * HEAD_DIM, (t + 1) * HEAD_DIM)

    order = [(c, o) for c in range(chunks) for o in range(n_mp)]

    def forward_send(m):
        query_raw = jnp.zeros((rows, inner_width), jnp.float32)
        squares = jnp.zeros((rows, 1), jnp.float32)
        for c, o in order:
            h = lax.rem(y + o, n_mp)

            @pl.when(jnp.logical_not(first))
            def _():
                relay_copy(xsend, xbuf, s_x, r_x, m, c, h, {"mp": y}, 0).wait_recv()

            x = xbuf[m, h, c]
            x_float = x.astype(jnp.float32)
            squares += jnp.sum(x_float * x_float, axis=-1, keepdims=True)
            query_raw += dot(x, wq[h * chunks + c])
        scale_r = lax.rsqrt(squares / width + 1e-06)
        query = (query_raw * scale_r).astype(jnp.bfloat16)
        rbuf[m] = jnp.broadcast_to(scale_r, rbuf.shape[1:])
        qbuf[m] = query
        live = mask[...] > 0
        parts = []
        for t in range(heads):
            scores = dot(query[:, head(t)], kv[0, :, head(t)], NT) * scale
            scores = jnp.where(live, scores, -1e30)
            top = jnp.max(scores, axis=-1, keepdims=True)
            powers = jnp.exp(scores - top)
            prob = powers / jnp.sum(powers, axis=-1, keepdims=True)
            prob_buf[m, t] = prob
            parts.append(dot(prob.astype(jnp.bfloat16), kv[1, :, head(t)]).astype(jnp.bfloat16))
        attended = jnp.concatenate(parts, axis=1)
        att_all[z, group_rows(m)] = attended
        for o in range(1, n_mp):
            h = lax.rem(y + o, n_mp)
            for c in range(chunks):
                piece = dot(attended, wo[:, columns(h * chunks + c)])
                psend[m, o - 1, c] = piece.astype(jnp.bfloat16)
                share_copy(psend, precv, s_p, r_p, m, c, o).start()

        @pl.loop(1, n_dp)
        def _(k):
            att_copy(m, k, z).start()

        for c in range(chunks):
            own[c] = dot(attended, wo[:, columns(y * chunks + c)])

    def forward_finish(m):
        for c in range(chunks):
            total = own[c]
            for o in range(1, n_mp):
                share_copy(psend, precv, s_p, r_p, m, c, o).wait_recv()
                total += precv[m, o - 1, c].astype(jnp.float32)
            x_float = xbuf[m, y, c].astype(jnp.float32)
            result = (x_float + gate[y * chunks + c] * total).astype(jnp.bfloat16)
            xsend[m, c] = result

            @pl.when(jnp.logical_not(last))
            def _():
                for o in reversed(range(n_mp)):
                    forward_copy(m, c, o).start()

            out_ref[m, :, c * chunk : (c + 1) * chunk] = result

    def backward_send(m):
        d_att = jnp.zeros((rows, inner_width), jnp.float32)
        for c, o in order:
            h = lax.rem(y + o, n_mp)
            j = h * chunks + c

            @pl.when(jnp.logical_not(last))
            def _():
                relay_copy(dxsend, dybuf, s_dy, r_dy, m, c, h, {"mp": y}, 0).wait_recv()

            dproj = (gate[j] * dybuf[m, h, c].astype(jnp.float32)).astype(jnp.bfloat16)
            for t in range(slabs):
                dpj[j * slabs + t, group_rows(m)] = dproj[:, t * share : (t + 1) * share]
            d_att += dot(dproj, wo[:, columns(j)], NT)

        @pl.loop(1, n_dp)
        def _(k):
            dproj_copy(m, k, z, lax.rem(z + k, n_dp)).start()

        d_att = d_att.astype(jnp.bfloat16)
        query = qbuf[m]
        inner = jnp.zeros((rows, 1), jnp.float32)
        parts = []
        for t in range(heads):
            prob = prob_buf[m, t]
            d_prob = dot(d_att[:, head(t)], kv[1, :, head(t)], NT)
            mean = jnp.sum(prob * d_prob, axis=-1, keepdims=True)
            d_score = (prob * (d_prob - mean)).astype(jnp.bfloat16)
            d_query = (dot(d_score, kv[0, :, head(t)]) * scale).astype(jnp.bfloat16)
            both = d_query.astype(jnp.float32) * query[:, head(t)].astype(jnp.float32)
            inner += jnp.sum(both, axis=-1, keepdims=True)
            parts.append(d_query)
        d_query = jnp.concatenate(parts, axis=1)
        pull = rbuf[m][:, :1] * inner / width

        def piece_of(h, c):
            x_float = xbuf[m, h, c].astype(jnp.float32)
            return dot(d_query, wq[h * chunks + c], NT) - x_float * pull

        for o in range(1, n_mp):
            h = lax.rem(y + o, n_mp)
            for c in range(chunks):
                bsend[m, o - 1, c] = piece_of(h, c).astype(jnp.bfloat16)
                share_copy(bsend, brecv, s_b, r_b, m, c, o).start()
        for c in range(chunks):
            own[c] = piece_of(y, c)

    def backward_finish(m):
        scale_r = rbuf[m][:, :1]
        for c in range(chunks):
            total = own[c]
            for o in range(1, n_mp):
                share_copy(bsend, brecv, s_b, r_b, m, c, o).wait_recv()
                total += brecv[m, o - 1, c].astype(jnp.float32)
            dy = dybuf[m, y, c].astype(jnp.float32)
            result = (dy + scale_r * total).astype(jnp.bfloat16)
            dxsend[m, c] = result

            @pl.when(jnp.logical_not(first))
            def _():
                for o in reversed(range(n_mp)):
                    backward_copy(m, c, o).start()

            dx_ref[m, :, c * chunk : (c + 1) * chunk] = result

    @pl.loop(0, groups)
    def _(m):
        forward_send(m)
        forward_finish(m)

    @pl.loop(0, groups)
    def _(m):
        backward_send(m)
        backward_finish(m)

    dcol[z] = dpj[z]

    @pl.loop(0, groups)
    def _(m):
        @pl.loop(1, n_dp)
        def _(k):
            source = lax.rem(z + n_dp - k, n_dp)
            att_copy(m, k, source).wait_recv()
            dproj_copy(m, k, source, z).wait_recv()

    depth = n_dp * groups * rows
    for t in range(heads // 2):
        cut = slice(2 * t * HEAD_DIM, 2 * (t + 1) * HEAD_DIM)
        left = att_all[:, :, cut].reshape(depth, 2 * HEAD_DIM)
        wg_ref[cut, :] = dot(left, dcol[...].reshape(depth, share), TN)

    @pl.loop(0, groups)
    def _(m):
        @pl.loop(1, n_dp)
        def _(k):
            att_copy(m, k, z).wait_send()
            dproj_copy(m, k, z, lax.rem(z + k, n_dp)).wait_send()

        for c in range(chunks):
            for o in range(1, n_mp):
                share_copy(psend, precv, s_p, r_p, m, c, o).wait_send()
                share_copy(bsend, brecv, s_b, r_b, m, c, o).wait_send()

            @pl.when(jnp.logical_not(last))
            def _():
                for o in range(n_mp):
                    forward_copy(m, c, o).wait_send()

            @pl.when(jnp.logical_not(first))
            def _():
                for o in range(n_mp):
                    backward_copy(m, c, o).wait_send()


def per_device(latents, caption_kv, caption_mask, query_weight, out_weight, gate, cotangent):
    micro, tok, width = latents.shape[1:]
    n_dp, n_pipe, n_mp = (lax.axis_size("dp"), lax.axis_size("pipe"), lax.axis_size("mp"))
    total_rows = micro * tok
    rows = total_rows // GROUPS
    half = width // n_mp
    chunk = half // CHUNKS
    inner_width = out_weight.shape[1]
    heads = inner_width // HEAD_DIM
    cap = caption_mask.shape[1]
    share = width // n_dp
    bf16, f32 = (jnp.bfloat16, jnp.float32)
    whole = (GROUPS, n_mp, CHUNKS, rows, chunk)
    mine = (GROUPS, CHUNKS, rows, chunk)
    cross = (GROUPS, n_mp - 1, CHUNKS, rows, chunk)
    sem = pltpu.SemaphoreType.DMA
    vmem = pl.BlockSpec(memory_space=pltpu.VMEM)
    section_out, input_grad, weight_grad = pl.pallas_call(
        functools.partial(relay_kernel, (n_dp, n_pipe, n_mp)),
        out_shape=(
            jax.ShapeDtypeStruct((GROUPS, rows, half), bf16),
            jax.ShapeDtypeStruct((GROUPS, rows, half), bf16),
            jax.ShapeDtypeStruct((inner_width, share), f32),
        ),
        in_specs=[vmem] * 7,
        out_specs=(vmem,) * 3,
        scratch_shapes=[
            pltpu.VMEM(whole, bf16),
            pltpu.VMEM(whole, bf16),
            pltpu.VMEM(mine, bf16),
            pltpu.VMEM(mine, bf16),
            pltpu.VMEM(cross, bf16),
            pltpu.VMEM(cross, bf16),
            pltpu.VMEM(cross, bf16),
            pltpu.VMEM(cross, bf16),
            pltpu.VMEM(mine[1:], f32),
            pltpu.VMEM((GROUPS, heads, rows, cap), f32),
            pltpu.VMEM((GROUPS, rows, inner_width), bf16),
            pltpu.VMEM((GROUPS, rows, 128), f32),
            pltpu.VMEM((n_dp, total_rows, inner_width), bf16),
            pltpu.VMEM((n_dp, total_rows, share), bf16),
            pltpu.VMEM((n_dp, total_rows, share), bf16),
            sem((GROUPS, CHUNKS, n_mp)),
            sem((GROUPS, n_mp, CHUNKS)),
            sem((GROUPS, CHUNKS, n_mp)),
            sem((GROUPS, n_mp, CHUNKS)),
            sem((GROUPS, n_mp - 1, CHUNKS)),
            sem((GROUPS, n_mp - 1, CHUNKS)),
            sem((GROUPS, n_mp - 1, CHUNKS)),
            sem((GROUPS, n_mp - 1, CHUNKS)),
            sem((GROUPS, n_dp)),
            sem((GROUPS, n_dp)),
            sem((GROUPS, n_dp)),
            sem((GROUPS, n_dp)),
        ],
        compiler_params=pltpu.CompilerParams(
            collective_id=0, has_side_effects=True, vmem_limit_bytes=56 * 2**20
        ),
        name="relay",
    )(
        latents.reshape(GROUPS, rows, width),
        caption_kv[0, 0],
        caption_mask,
        query_weight.reshape(n_mp * CHUNKS, chunk, inner_width),
        out_weight[0],
        gate.reshape(n_mp * CHUNKS, 1, chunk),
        cotangent.reshape(GROUPS, rows, width),
    )
    shape = (1, 1, micro, tok, half)
    return (section_out.reshape(shape), input_grad.reshape(shape), weight_grad[None])


def solution(mesh):
    return jax.shard_map(
        per_device,
        mesh=mesh,
        in_specs=(
            P("dp", None, None, None),
            P("dp", "pipe", None, None, "mp"),
            P("dp", None),
            P("pipe", None, "mp"),
            P("pipe", "mp", None),
            P("pipe", None),
            P("dp", None, None, None),
        ),
        out_specs=(
            P("pipe", "dp", None, None, "mp"),
            P("pipe", "dp", None, None, "mp"),
            P("pipe", "mp", "dp"),
        ),
        check_vma=False,
    )
```

```python
import functools
import math

import jax
import jax.numpy as jnp
from jax import lax
from jax.experimental import pallas as pl
from jax.experimental.pallas import tpu as pltpu
from jax.sharding import PartitionSpec as P

HEAD_DIM = 128
GROUPS = 2
CHUNKS = 2
MESH = pl.DeviceIdType.MESH
NT = (((1,), (1,)), ((), ()))
TN = (((0,), (0,)), ((), ()))


def dot(a, b, dims=(((1,), (0,)), ((), ()))):
    return lax.dot_general(a, b, dims, preferred_element_type=jnp.float32)


def relay_kernel(
    sizes,
    lat,
    kv_any,
    mask,
    wq_any,
    wo_any,
    gate,
    cot,
    out_ref,
    dx_ref,
    att_all,
    dcol,
    kv,
    wq,
    wo,
    xbuf,
    dybuf,
    xsend,
    dxsend,
    psend,
    precv,
    bsend,
    brecv,
    own,
    prob_buf,
    qbuf,
    rbuf,
    dqbuf,
    pbuf,
    dpj,
    s_w,
    s_x,
    r_x,
    s_dy,
    r_dy,
    s_p,
    r_p,
    s_b,
    r_b,
    s_att,
    r_att,
    s_dp,
    r_dp,
):
    n_dp, n_pipe, n_mp = sizes
    groups, rows, width = lat.shape
    chunks, chunk = (xbuf.shape[2], xbuf.shape[4])
    inner_width = wo.shape[0]
    heads = inner_width // HEAD_DIM
    share = dpj.shape[2]
    slabs = chunk // share
    scale = 1.0 / math.sqrt(HEAD_DIM)
    z = lax.axis_index("dp")
    p = lax.axis_index("pipe")
    y = lax.axis_index("mp")
    first = p == 0
    last = p == n_pipe - 1

    def load(i, src, dst):
        return pltpu.make_async_copy(src, dst, s_w.at[i])

    load_wq = load(0, wq_any, wq)
    load_kv = load(1, kv_any, kv)
    load_wo = load(2, wo_any, wo)

    def load_rows(src, dst, sems):
        for m in range(groups):
            for c in range(chunks):
                for h in range(n_mp):
                    begin = (h * chunks + c) * chunk
                    pltpu.make_async_copy(
                        src.at[m, :, pl.ds(begin, chunk)], dst.at[m, h, c], sems.at[m, h, c]
                    ).start()

    @pl.when(first)
    def _():
        load_rows(lat, xbuf, r_x)

    load_wq.start()
    load_kv.start()
    load_wo.start()

    @pl.when(last)
    def _():
        load_rows(cot, dybuf, r_dy)

    barrier = pltpu.get_barrier_semaphore()

    def greet(target):
        pl.semaphore_signal(barrier, inc=1, device_id=target, device_id_type=MESH)

    for o in range(1, n_mp):
        greet({"mp": lax.rem(y + o, n_mp)})

    @pl.loop(1, n_dp)
    def _(k):
        greet({"dp": lax.rem(z + k, n_dp)})

    @pl.when(jnp.logical_not(first))
    def _():
        for h in range(n_mp):
            greet({"pipe": p - 1, "mp": h})

    @pl.when(jnp.logical_not(last))
    def _():
        for h in range(n_mp):
            greet({"pipe": p + 1, "mp": h})

    edges = first.astype(jnp.int32) + last.astype(jnp.int32)
    pl.semaphore_wait(barrier, (n_mp - 1) + (n_dp - 1) + n_mp * (2 - edges))

    def group_rows(m):
        return pl.ds(pl.multiple_of(m * rows, rows), rows)

    def columns(j):
        return pl.ds(pl.multiple_of(j * chunk, 128), chunk)

    def relay_copy(src, dst, send, recv, m, c, h, target, slot):
        return pltpu.make_async_remote_copy(
            src_ref=src.at[m, c],
            dst_ref=dst.at[m, h, c],
            send_sem=send.at[m, c, slot],
            recv_sem=recv.at[m, h, c],
            device_id=target,
            device_id_type=MESH,
        )

    def forward_copy(m, c, o):
        target = {"pipe": p + 1, "mp": lax.rem(y + o, n_mp)}
        return relay_copy(xsend, xbuf, s_x, r_x, m, c, y, target, o)

    def backward_copy(m, c, o):
        target = {"pipe": p - 1, "mp": lax.rem(y + o, n_mp)}
        return relay_copy(dxsend, dybuf, s_dy, r_dy, m, c, y, target, o)

    def share_copy(src, dst, send, recv, m, c, o):
        return pltpu.make_async_remote_copy(
            src_ref=src.at[m, o - 1, c],
            dst_ref=dst.at[m, o - 1, c],
            send_sem=send.at[m, o - 1, c],
            recv_sem=recv.at[m, o - 1, c],
            device_id={"mp": lax.rem(y + o, n_mp)},
            device_id_type=MESH,
        )

    def att_copy(m, k, source):
        piece = att_all.at[source, group_rows(m)]
        return pltpu.make_async_remote_copy(
            src_ref=piece,
            dst_ref=piece,
            send_sem=s_att.at[m, k],
            recv_sem=r_att.at[m, k],
            device_id={"dp": lax.rem(z + k, n_dp)},
            device_id_type=MESH,
        )

    def dproj_copy(m, k, source, owner):
        return pltpu.make_async_remote_copy(
            src_ref=dpj.at[owner, group_rows(m)],
            dst_ref=dcol.at[source, group_rows(m)],
            send_sem=s_dp.at[m, k],
            recv_sem=r_dp.at[m, k],
            device_id={"dp": lax.rem(z + k, n_dp)},
            device_id_type=MESH,
        )

    def head(t):
        return slice(t * HEAD_DIM, (t + 1) * HEAD_DIM)

    order = [(c, o) for c in range(chunks) for o in range(n_mp)]

    def forward_query(m):
        query_raw = jnp.zeros((rows, inner_width), jnp.float32)
        squares = jnp.zeros((rows, 1), jnp.float32)
        for c, o in order:
            h = lax.rem(y + o, n_mp)

            relay_copy(xsend, xbuf, s_x, r_x, m, c, h, {"mp": y}, 0).wait_recv()
            x = xbuf[m, h, c]
            x_float = x.astype(jnp.float32)
            squares += jnp.sum(x_float * x_float, axis=-1, keepdims=True)
            query_raw += dot(x, wq[h * chunks + c])
        scale_r = lax.rsqrt(squares / width + 1e-06)
        query = (query_raw * scale_r).astype(jnp.bfloat16)
        rbuf[m] = jnp.broadcast_to(scale_r, rbuf.shape[1:])
        qbuf[m] = query
        live = mask[...] > 0
        parts = []
        for t in range(heads):
            scores = dot(query[:, head(t)], kv[0, :, head(t)], NT) * scale
            scores = jnp.where(live, scores, -1e30)
            top = jnp.max(scores, axis=-1, keepdims=True)
            powers = jnp.exp(scores - top)
            prob = powers / jnp.sum(powers, axis=-1, keepdims=True)
            prob_buf[m, t] = prob
            parts.append(dot(prob.astype(jnp.bfloat16), kv[1, :, head(t)]).astype(jnp.bfloat16))
        attended = jnp.concatenate(parts, axis=1)
        att_all[z, group_rows(m)] = attended

        @pl.loop(1, n_dp)
        def _(k):
            att_copy(m, k, z).start()

    def forward_share(m):
        attended = att_all[z, group_rows(m)]
        for o in range(1, n_mp):
            h = lax.rem(y + o, n_mp)
            for c in range(chunks):
                piece = dot(attended, wo[:, columns(h * chunks + c)])
                psend[m, o - 1, c] = piece.astype(jnp.bfloat16)
                share_copy(psend, precv, s_p, r_p, m, c, o).start()
        for c in range(chunks):
            own[0, m, c] = dot(attended, wo[:, columns(y * chunks + c)])

    def forward_finish(m):
        for c in range(chunks):
            total = own[0, m, c]
            for o in range(1, n_mp):
                share_copy(psend, precv, s_p, r_p, m, c, o).wait_recv()
                total += precv[m, o - 1, c].astype(jnp.float32)
            x_float = xbuf[m, y, c].astype(jnp.float32)
            result = (x_float + gate[y * chunks + c] * total).astype(jnp.bfloat16)
            xsend[m, c] = result

            @pl.when(jnp.logical_not(last))
            def _():
                for o in reversed(range(n_mp)):
                    forward_copy(m, c, o).start()

            out_ref[m, :, c * chunk : (c + 1) * chunk] = result

    def backward_query(m):
        d_att = jnp.zeros((rows, inner_width), jnp.float32)
        for c, o in order:
            h = lax.rem(y + o, n_mp)
            j = h * chunks + c

            relay_copy(dxsend, dybuf, s_dy, r_dy, m, c, h, {"mp": y}, 0).wait_recv()
            dproj = (gate[j] * dybuf[m, h, c].astype(jnp.float32)).astype(jnp.bfloat16)
            for t in range(slabs):
                dpj[j * slabs + t, group_rows(m)] = dproj[:, t * share : (t + 1) * share]
            d_att += dot(dproj, wo[:, columns(j)], NT)

        @pl.loop(1, n_dp)
        def _(k):
            dproj_copy(m, k, z, lax.rem(z + k, n_dp)).start()

        d_att = d_att.astype(jnp.bfloat16)
        query = qbuf[m]
        inner = jnp.zeros((rows, 1), jnp.float32)
        parts = []
        for t in range(heads):
            prob = prob_buf[m, t]
            d_prob = dot(d_att[:, head(t)], kv[1, :, head(t)], NT)
            mean = jnp.sum(prob * d_prob, axis=-1, keepdims=True)
            d_score = (prob * (d_prob - mean)).astype(jnp.bfloat16)
            d_query = (dot(d_score, kv[0, :, head(t)]) * scale).astype(jnp.bfloat16)
            both = d_query.astype(jnp.float32) * query[:, head(t)].astype(jnp.float32)
            inner += jnp.sum(both, axis=-1, keepdims=True)
            parts.append(d_query)
        dqbuf[m] = jnp.concatenate(parts, axis=1)
        pbuf[m] = jnp.broadcast_to(rbuf[m][:, :1] * inner / width, pbuf.shape[1:])

    def backward_share(m):
        d_query = dqbuf[m]
        pull = pbuf[m][:, :1]

        def piece_of(h, c):
            x_float = xbuf[m, h, c].astype(jnp.float32)
            return dot(d_query, wq[h * chunks + c], NT) - x_float * pull

        for o in range(1, n_mp):
            h = lax.rem(y + o, n_mp)
            for c in range(chunks):
                bsend[m, o - 1, c] = piece_of(h, c).astype(jnp.bfloat16)
                share_copy(bsend, brecv, s_b, r_b, m, c, o).start()
        for c in range(chunks):
            own[1, m, c] = piece_of(y, c)

    def backward_finish(m):
        scale_r = rbuf[m][:, :1]
        for c in range(chunks):
            total = own[1, m, c]
            for o in range(1, n_mp):
                share_copy(bsend, brecv, s_b, r_b, m, c, o).wait_recv()
                total += brecv[m, o - 1, c].astype(jnp.float32)
            dy = dybuf[m, y, c].astype(jnp.float32)
            result = (dy + scale_r * total).astype(jnp.bfloat16)
            dxsend[m, c] = result

            @pl.when(jnp.logical_not(first))
            def _():
                for o in reversed(range(n_mp)):
                    backward_copy(m, c, o).start()

            dx_ref[m, :, c * chunk : (c + 1) * chunk] = result

    late = last.astype(jnp.int32)
    turn = groups * (1 - late)
    held_back = (groups + 1) * late

    load_wq.wait()
    load_kv.wait()

    @pl.loop(0, 2 * groups + 2)
    def _(step):
        def phase(run, m):
            @pl.when(jnp.logical_and(m >= 0, m < groups))
            def _():
                run(m)

        phase(forward_query, step)

        @pl.when(step == 0)
        def _():
            load_wo.wait()

        phase(forward_finish, step - held_back - 1)
        phase(forward_share, step - held_back)
        phase(backward_query, step - turn)
        phase(backward_finish, step - turn - 1)
        phase(backward_share, step - turn)

    dcol[z] = dpj[z]

    @pl.loop(0, groups)
    def _(m):
        @pl.loop(1, n_dp)
        def _(k):
            source = lax.rem(z + n_dp - k, n_dp)
            att_copy(m, k, source).wait_recv()
            dproj_copy(m, k, source, z).wait_recv()

    @pl.loop(0, groups)
    def _(m):
        @pl.loop(1, n_dp)
        def _(k):
            att_copy(m, k, z).wait_send()
            dproj_copy(m, k, z, lax.rem(z + k, n_dp)).wait_send()

        for c in range(chunks):
            for o in range(1, n_mp):
                share_copy(psend, precv, s_p, r_p, m, c, o).wait_send()
                share_copy(bsend, brecv, s_b, r_b, m, c, o).wait_send()

            @pl.when(jnp.logical_not(last))
            def _():
                for o in range(n_mp):
                    forward_copy(m, c, o).wait_send()

            @pl.when(jnp.logical_not(first))
            def _():
                for o in range(n_mp):
                    backward_copy(m, c, o).wait_send()


def result_kernel(att, dproj, out, dx, out_ref, dx_ref, wg_ref):
    depth = att.shape[0] * att.shape[1]
    left = att[...].reshape(depth, att.shape[2])
    wg_ref[...] = dot(left, dproj[...].reshape(depth, dproj.shape[2]), TN)
    out_ref[...] = out[...]
    dx_ref[...] = dx[...]


def per_device(latents, caption_kv, caption_mask, query_weight, out_weight, gate, cotangent):
    micro, tok, width = latents.shape[1:]
    n_dp, n_pipe, n_mp = (lax.axis_size("dp"), lax.axis_size("pipe"), lax.axis_size("mp"))
    total_rows = micro * tok
    rows = total_rows // GROUPS
    half = width // n_mp
    chunk = half // CHUNKS
    inner_width = out_weight.shape[1]
    heads = inner_width // HEAD_DIM
    cap = caption_mask.shape[1]
    share = width // n_dp
    bf16, f32 = (jnp.bfloat16, jnp.float32)
    whole = (GROUPS, n_mp, CHUNKS, rows, chunk)
    mine = (GROUPS, CHUNKS, rows, chunk)
    cross = (GROUPS, n_mp - 1, CHUNKS, rows, chunk)
    sem = pltpu.SemaphoreType.DMA
    vmem = pl.BlockSpec(memory_space=pltpu.VMEM)
    anywhere = pl.BlockSpec(memory_space=pl.ANY)
    section_out, input_grad, attended, dproj = pl.pallas_call(
        functools.partial(relay_kernel, (n_dp, n_pipe, n_mp)),
        out_shape=(
            jax.ShapeDtypeStruct((GROUPS, rows, half), bf16),
            jax.ShapeDtypeStruct((GROUPS, rows, half), bf16),
            jax.ShapeDtypeStruct((n_dp, total_rows, inner_width), bf16),
            jax.ShapeDtypeStruct((n_dp, total_rows, share), bf16),
        ),
        in_specs=[anywhere, anywhere, vmem, anywhere, anywhere, vmem, anywhere],
        out_specs=(vmem,) * 4,
        scratch_shapes=[
            pltpu.VMEM(caption_kv.shape[2:], bf16),
            pltpu.VMEM((n_mp * CHUNKS, chunk, inner_width), bf16),
            pltpu.VMEM(out_weight.shape[1:], bf16),
            pltpu.VMEM(whole, bf16),
            pltpu.VMEM(whole, bf16),
            pltpu.VMEM(mine, bf16),
            pltpu.VMEM(mine, bf16),
            pltpu.VMEM(cross, bf16),
            pltpu.VMEM(cross, bf16),
            pltpu.VMEM(cross, bf16),
            pltpu.VMEM(cross, bf16),
            pltpu.VMEM((2,) + mine, f32),
            pltpu.VMEM((GROUPS, heads, rows, cap), f32),
            pltpu.VMEM((GROUPS, rows, inner_width), bf16),
            pltpu.VMEM((GROUPS, rows, 128), f32),
            pltpu.VMEM((GROUPS, rows, inner_width), bf16),
            pltpu.VMEM((GROUPS, rows, 128), f32),
            pltpu.VMEM((n_dp, total_rows, share), bf16),
            sem((3,)),
            sem((GROUPS, CHUNKS, n_mp)),
            sem((GROUPS, n_mp, CHUNKS)),
            sem((GROUPS, CHUNKS, n_mp)),
            sem((GROUPS, n_mp, CHUNKS)),
            sem((GROUPS, n_mp - 1, CHUNKS)),
            sem((GROUPS, n_mp - 1, CHUNKS)),
            sem((GROUPS, n_mp - 1, CHUNKS)),
            sem((GROUPS, n_mp - 1, CHUNKS)),
            sem((GROUPS, n_dp)),
            sem((GROUPS, n_dp)),
            sem((GROUPS, n_dp)),
            sem((GROUPS, n_dp)),
        ],
        compiler_params=pltpu.CompilerParams(
            collective_id=0, has_side_effects=True, vmem_limit_bytes=56 * 2**20
        ),
        name="relay",
    )(
        latents.reshape(GROUPS, rows, width),
        caption_kv[0, 0],
        caption_mask,
        query_weight.reshape(n_mp * CHUNKS, chunk, inner_width),
        out_weight[0],
        gate.reshape(n_mp * CHUNKS, 1, chunk),
        cotangent.reshape(GROUPS, rows, width),
    )
    tiles = heads // 2 if heads % 2 == 0 and half % (heads // 2 * 128) == 0 else 1
    part = inner_width // tiles
    band = pl.BlockSpec((GROUPS, rows, half // tiles), lambda i: (0, 0, i))
    section_out, input_grad, weight_grad = pl.pallas_call(
        result_kernel,
        grid=(tiles,),
        out_shape=(
            jax.ShapeDtypeStruct((GROUPS, rows, half), bf16),
            jax.ShapeDtypeStruct((GROUPS, rows, half), bf16),
            jax.ShapeDtypeStruct((inner_width, share), f32),
        ),
        in_specs=[
            pl.BlockSpec((n_dp, total_rows, part), lambda i: (0, 0, i)),
            pl.BlockSpec((n_dp, total_rows, share), lambda i: (0, 0, 0)),
            band,
            band,
        ],
        out_specs=(band, band, pl.BlockSpec((part, share), lambda i: (i, 0))),
        compiler_params=pltpu.CompilerParams(vmem_limit_bytes=56 * 2**20),
        name="results",
    )(attended, dproj, section_out, input_grad)
    shape = (1, 1, micro, tok, half)
    return (section_out.reshape(shape), input_grad.reshape(shape), weight_grad[None])


def solution(mesh):
    return jax.shard_map(
        per_device,
        mesh=mesh,
        in_specs=(
            P("dp", None, None, None),
            P("dp", "pipe", None, None, "mp"),
            P("dp", None),
            P("pipe", None, "mp"),
            P("pipe", "mp", None),
            P("pipe", None),
            P("dp", None, None, None),
        ),
        out_specs=(
            P("pipe", "dp", None, None, "mp"),
            P("pipe", "dp", None, None, "mp"),
            P("pipe", "mp", "dp"),
        ),
        check_vma=False,
    )
```

```python
import functools
import math

import jax
import jax.numpy as jnp
from jax import lax
from jax.experimental import pallas as pl
from jax.experimental.pallas import tpu as pltpu
from jax.sharding import PartitionSpec as P

HEAD_DIM = 128
GROUPS = 4
CHUNKS = 2
MESH = pl.DeviceIdType.MESH
NT = (((1,), (1,)), ((), ()))
TN = (((0,), (0,)), ((), ()))


def dot(a, b, dims=(((1,), (0,)), ((), ()))):
    return lax.dot_general(a, b, dims, preferred_element_type=jnp.float32)


def relay_kernel(
    sizes,
    lat,
    kv_any,
    mask,
    wq_any,
    wo_any,
    gate,
    cot,
    out_ref,
    dx_ref,
    att_all,
    dcol,
    kv,
    wq,
    wo,
    xbuf,
    dybuf,
    xsend,
    dxsend,
    psend,
    precv,
    bsend,
    brecv,
    own,
    prob_buf,
    qbuf,
    rbuf,
    dqbuf,
    pbuf,
    dpj,
    s_w,
    s_x,
    r_x,
    s_dy,
    r_dy,
    s_p,
    r_p,
    s_b,
    r_b,
    s_att,
    r_att,
    s_dp,
    r_dp,
):
    n_dp, n_pipe, n_mp = sizes
    groups, rows, width = lat.shape
    chunks, chunk = (xbuf.shape[2], xbuf.shape[4])
    inner_width = wo.shape[0]
    heads = inner_width // HEAD_DIM
    share = dpj.shape[2]
    slabs = chunk // share
    scale = 1.0 / math.sqrt(HEAD_DIM)
    z = lax.axis_index("dp")
    p = lax.axis_index("pipe")
    y = lax.axis_index("mp")
    first = p == 0
    last = p == n_pipe - 1

    def load(i, src, dst):
        return pltpu.make_async_copy(src, dst, s_w.at[i])

    load_wq = load(0, wq_any, wq)
    load_kv = load(1, kv_any, kv)
    load_wo = load(2, wo_any, wo)

    def load_rows(src, dst, sems):
        for m in range(groups):
            for c in range(chunks):
                for h in range(n_mp):
                    begin = (h * chunks + c) * chunk
                    pltpu.make_async_copy(
                        src.at[m, :, pl.ds(begin, chunk)], dst.at[m, h, c], sems.at[m, h, c]
                    ).start()

    @pl.when(first)
    def _():
        load_rows(lat, xbuf, r_x)

    load_wq.start()
    load_kv.start()
    load_wo.start()

    @pl.when(last)
    def _():
        load_rows(cot, dybuf, r_dy)

    barrier = pltpu.get_barrier_semaphore()

    def greet(target):
        pl.semaphore_signal(barrier, inc=1, device_id=target, device_id_type=MESH)

    for o in range(1, n_mp):
        greet({"mp": lax.rem(y + o, n_mp)})

    @pl.loop(1, n_dp)
    def _(k):
        greet({"dp": lax.rem(z + k, n_dp)})

    @pl.when(jnp.logical_not(first))
    def _():
        for h in range(n_mp):
            greet({"pipe": p - 1, "mp": h})

    @pl.when(jnp.logical_not(last))
    def _():
        for h in range(n_mp):
            greet({"pipe": p + 1, "mp": h})

    edges = first.astype(jnp.int32) + last.astype(jnp.int32)
    pl.semaphore_wait(barrier, (n_mp - 1) + (n_dp - 1) + n_mp * (2 - edges))

    def group_rows(m):
        return pl.ds(pl.multiple_of(m * rows, rows), rows)

    def columns(j):
        return pl.ds(pl.multiple_of(j * chunk, 128), chunk)

    def relay_copy(src, dst, send, recv, m, c, h, target, slot):
        return pltpu.make_async_remote_copy(
            src_ref=src.at[m, c],
            dst_ref=dst.at[m, h, c],
            send_sem=send.at[m, c, slot],
            recv_sem=recv.at[m, h, c],
            device_id=target,
            device_id_type=MESH,
        )

    def forward_copy(m, c, o):
        target = {"pipe": p + 1, "mp": lax.rem(y + o, n_mp)}
        return relay_copy(xsend, xbuf, s_x, r_x, m, c, y, target, o)

    def backward_copy(m, c, o):
        target = {"pipe": p - 1, "mp": lax.rem(y + o, n_mp)}
        return relay_copy(dxsend, dybuf, s_dy, r_dy, m, c, y, target, o)

    def share_copy(src, dst, send, recv, m, c, o):
        return pltpu.make_async_remote_copy(
            src_ref=src.at[m, o - 1, c],
            dst_ref=dst.at[m, o - 1, c],
            send_sem=send.at[m, o - 1, c],
            recv_sem=recv.at[m, o - 1, c],
            device_id={"mp": lax.rem(y + o, n_mp)},
            device_id_type=MESH,
        )

    def att_copy(m, k, source):
        piece = att_all.at[source, group_rows(m)]
        return pltpu.make_async_remote_copy(
            src_ref=piece,
            dst_ref=piece,
            send_sem=s_att.at[m, k],
            recv_sem=r_att.at[m, k],
            device_id={"dp": lax.rem(z + k, n_dp)},
            device_id_type=MESH,
        )

    def dproj_copy(m, k, source, owner):
        return pltpu.make_async_remote_copy(
            src_ref=dpj.at[owner, group_rows(m)],
            dst_ref=dcol.at[source, group_rows(m)],
            send_sem=s_dp.at[m, k],
            recv_sem=r_dp.at[m, k],
            device_id={"dp": lax.rem(z + k, n_dp)},
            device_id_type=MESH,
        )

    def head(t):
        return slice(t * HEAD_DIM, (t + 1) * HEAD_DIM)

    order = [(c, o) for c in range(chunks) for o in range(n_mp)]

    def forward_query(m):
        query_raw = jnp.zeros((rows, inner_width), jnp.float32)
        squares = jnp.zeros((rows, 1), jnp.float32)
        for c, o in order:
            h = lax.rem(y + o, n_mp)

            relay_copy(xsend, xbuf, s_x, r_x, m, c, h, {"mp": y}, 0).wait_recv()
            x = xbuf[m, h, c]
            x_float = x.astype(jnp.float32)
            squares += jnp.sum(x_float * x_float, axis=-1, keepdims=True)
            query_raw += dot(x, wq[h * chunks + c])
        scale_r = lax.rsqrt(squares / width + 1e-06)
        query = (query_raw * scale_r).astype(jnp.bfloat16)
        rbuf[m] = jnp.broadcast_to(scale_r, rbuf.shape[1:])
        qbuf[m] = query
        live = mask[...] > 0
        parts = []
        for t in range(heads):
            scores = dot(query[:, head(t)], kv[0, :, head(t)], NT) * scale
            scores = jnp.where(live, scores, -1e30)
            top = jnp.max(scores, axis=-1, keepdims=True)
            powers = jnp.exp(scores - top)
            prob = powers / jnp.sum(powers, axis=-1, keepdims=True)
            prob_buf[m, t] = prob
            parts.append(dot(prob.astype(jnp.bfloat16), kv[1, :, head(t)]).astype(jnp.bfloat16))
        attended = jnp.concatenate(parts, axis=1)
        att_all[z, group_rows(m)] = attended

        @pl.loop(1, n_dp)
        def _(k):
            att_copy(m, k, z).start()

    def forward_share(m):
        attended = att_all[z, group_rows(m)]
        for o in range(1, n_mp):
            h = lax.rem(y + o, n_mp)
            for c in range(chunks):
                piece = dot(attended, wo[:, columns(h * chunks + c)])
                psend[m, o - 1, c] = piece.astype(jnp.bfloat16)
                share_copy(psend, precv, s_p, r_p, m, c, o).start()
        for c in range(chunks):
            own[0, m, c] = dot(attended, wo[:, columns(y * chunks + c)])

    def forward_finish(m):
        for c in range(chunks):
            total = own[0, m, c]
            for o in range(1, n_mp):
                share_copy(psend, precv, s_p, r_p, m, c, o).wait_recv()
                total += precv[m, o - 1, c].astype(jnp.float32)
            x_float = xbuf[m, y, c].astype(jnp.float32)
            result = (x_float + gate[y * chunks + c] * total).astype(jnp.bfloat16)
            xsend[m, c] = result

            @pl.when(jnp.logical_not(last))
            def _():
                for o in reversed(range(n_mp)):
                    forward_copy(m, c, o).start()

            out_ref[m, :, c * chunk : (c + 1) * chunk] = result

    def backward_query(m):
        d_att = jnp.zeros((rows, inner_width), jnp.float32)
        for c, o in order:
            h = lax.rem(y + o, n_mp)
            j = h * chunks + c

            relay_copy(dxsend, dybuf, s_dy, r_dy, m, c, h, {"mp": y}, 0).wait_recv()
            dproj = (gate[j] * dybuf[m, h, c].astype(jnp.float32)).astype(jnp.bfloat16)
            for t in range(slabs):
                dpj[j * slabs + t, group_rows(m)] = dproj[:, t * share : (t + 1) * share]
            d_att += dot(dproj, wo[:, columns(j)], NT)

        @pl.loop(1, n_dp)
        def _(k):
            dproj_copy(m, k, z, lax.rem(z + k, n_dp)).start()

        d_att = d_att.astype(jnp.bfloat16)
        query = qbuf[m]
        inner = jnp.zeros((rows, 1), jnp.float32)
        parts = []
        for t in range(heads):
            prob = prob_buf[m, t]
            d_prob = dot(d_att[:, head(t)], kv[1, :, head(t)], NT)
            mean = jnp.sum(prob * d_prob, axis=-1, keepdims=True)
            d_score = (prob * (d_prob - mean)).astype(jnp.bfloat16)
            d_query = (dot(d_score, kv[0, :, head(t)]) * scale).astype(jnp.bfloat16)
            both = d_query.astype(jnp.float32) * query[:, head(t)].astype(jnp.float32)
            inner += jnp.sum(both, axis=-1, keepdims=True)
            parts.append(d_query)
        dqbuf[m] = jnp.concatenate(parts, axis=1)
        pbuf[m] = jnp.broadcast_to(rbuf[m][:, :1] * inner / width, pbuf.shape[1:])

    def backward_share(m):
        d_query = dqbuf[m]
        pull = pbuf[m][:, :1]

        def piece_of(h, c):
            x_float = xbuf[m, h, c].astype(jnp.float32)
            return dot(d_query, wq[h * chunks + c], NT) - x_float * pull

        for o in range(1, n_mp):
            h = lax.rem(y + o, n_mp)
            for c in range(chunks):
                bsend[m, o - 1, c] = piece_of(h, c).astype(jnp.bfloat16)
                share_copy(bsend, brecv, s_b, r_b, m, c, o).start()
        for c in range(chunks):
            own[1, m, c] = piece_of(y, c)

    def backward_finish(m):
        scale_r = rbuf[m][:, :1]
        for c in range(chunks):
            total = own[1, m, c]
            for o in range(1, n_mp):
                share_copy(bsend, brecv, s_b, r_b, m, c, o).wait_recv()
                total += brecv[m, o - 1, c].astype(jnp.float32)
            dy = dybuf[m, y, c].astype(jnp.float32)
            result = (dy + scale_r * total).astype(jnp.bfloat16)
            dxsend[m, c] = result

            @pl.when(jnp.logical_not(first))
            def _():
                for o in reversed(range(n_mp)):
                    backward_copy(m, c, o).start()

            dx_ref[m, :, c * chunk : (c + 1) * chunk] = result

    late = last.astype(jnp.int32)
    turn = groups * (1 - late)
    held_back = (groups + 1) * late

    load_wq.wait()
    load_kv.wait()

    @pl.loop(0, 2 * groups + 2)
    def _(step):
        def phase(run, m):
            @pl.when(jnp.logical_and(m >= 0, m < groups))
            def _():
                run(m)

        phase(forward_query, step)

        @pl.when(step == 0)
        def _():
            load_wo.wait()

        phase(forward_finish, step - held_back - 1)
        phase(forward_share, step - held_back)
        phase(backward_query, step - turn)
        phase(backward_finish, step - turn - 1)
        phase(backward_share, step - turn)

    dcol[z] = dpj[z]

    @pl.loop(0, groups)
    def _(m):
        @pl.loop(1, n_dp)
        def _(k):
            source = lax.rem(z + n_dp - k, n_dp)
            att_copy(m, k, source).wait_recv()
            dproj_copy(m, k, source, z).wait_recv()

    @pl.loop(0, groups)
    def _(m):
        @pl.loop(1, n_dp)
        def _(k):
            att_copy(m, k, z).wait_send()
            dproj_copy(m, k, z, lax.rem(z + k, n_dp)).wait_send()

        for c in range(chunks):
            for o in range(1, n_mp):
                share_copy(psend, precv, s_p, r_p, m, c, o).wait_send()
                share_copy(bsend, brecv, s_b, r_b, m, c, o).wait_send()

            @pl.when(jnp.logical_not(last))
            def _():
                for o in range(n_mp):
                    forward_copy(m, c, o).wait_send()

            @pl.when(jnp.logical_not(first))
            def _():
                for o in range(n_mp):
                    backward_copy(m, c, o).wait_send()


def result_kernel(att, dproj, out, dx, out_ref, dx_ref, wg_ref):
    depth = att.shape[0] * att.shape[1]
    left = att[...].reshape(depth, att.shape[2])
    wg_ref[...] = dot(left, dproj[...].reshape(depth, dproj.shape[2]), TN)
    out_ref[...] = out[...]
    dx_ref[...] = dx[...]


def per_device(latents, caption_kv, caption_mask, query_weight, out_weight, gate, cotangent):
    micro, tok, width = latents.shape[1:]
    n_dp, n_pipe, n_mp = (lax.axis_size("dp"), lax.axis_size("pipe"), lax.axis_size("mp"))
    total_rows = micro * tok
    rows = total_rows // GROUPS
    half = width // n_mp
    chunk = half // CHUNKS
    inner_width = out_weight.shape[1]
    heads = inner_width // HEAD_DIM
    cap = caption_mask.shape[1]
    share = width // n_dp
    bf16, f32 = (jnp.bfloat16, jnp.float32)
    whole = (GROUPS, n_mp, CHUNKS, rows, chunk)
    mine = (GROUPS, CHUNKS, rows, chunk)
    cross = (GROUPS, n_mp - 1, CHUNKS, rows, chunk)
    sem = pltpu.SemaphoreType.DMA
    vmem = pl.BlockSpec(memory_space=pltpu.VMEM)
    anywhere = pl.BlockSpec(memory_space=pl.ANY)
    section_out, input_grad, attended, dproj = pl.pallas_call(
        functools.partial(relay_kernel, (n_dp, n_pipe, n_mp)),
        out_shape=(
            jax.ShapeDtypeStruct((GROUPS, rows, half), bf16),
            jax.ShapeDtypeStruct((GROUPS, rows, half), bf16),
            jax.ShapeDtypeStruct((n_dp, total_rows, inner_width), bf16),
            jax.ShapeDtypeStruct((n_dp, total_rows, share), bf16),
        ),
        in_specs=[anywhere, anywhere, vmem, anywhere, anywhere, vmem, anywhere],
        out_specs=(vmem,) * 4,
        scratch_shapes=[
            pltpu.VMEM(caption_kv.shape[2:], bf16),
            pltpu.VMEM((n_mp * CHUNKS, chunk, inner_width), bf16),
            pltpu.VMEM(out_weight.shape[1:], bf16),
            pltpu.VMEM(whole, bf16),
            pltpu.VMEM(whole, bf16),
            pltpu.VMEM(mine, bf16),
            pltpu.VMEM(mine, bf16),
            pltpu.VMEM(cross, bf16),
            pltpu.VMEM(cross, bf16),
            pltpu.VMEM(cross, bf16),
            pltpu.VMEM(cross, bf16),
            pltpu.VMEM((2,) + mine, f32),
            pltpu.VMEM((GROUPS, heads, rows, cap), f32),
            pltpu.VMEM((GROUPS, rows, inner_width), bf16),
            pltpu.VMEM((GROUPS, rows, 128), f32),
            pltpu.VMEM((GROUPS, rows, inner_width), bf16),
            pltpu.VMEM((GROUPS, rows, 128), f32),
            pltpu.VMEM((n_dp, total_rows, share), bf16),
            sem((3,)),
            sem((GROUPS, CHUNKS, n_mp)),
            sem((GROUPS, n_mp, CHUNKS)),
            sem((GROUPS, CHUNKS, n_mp)),
            sem((GROUPS, n_mp, CHUNKS)),
            sem((GROUPS, n_mp - 1, CHUNKS)),
            sem((GROUPS, n_mp - 1, CHUNKS)),
            sem((GROUPS, n_mp - 1, CHUNKS)),
            sem((GROUPS, n_mp - 1, CHUNKS)),
            sem((GROUPS, n_dp)),
            sem((GROUPS, n_dp)),
            sem((GROUPS, n_dp)),
            sem((GROUPS, n_dp)),
        ],
        compiler_params=pltpu.CompilerParams(
            collective_id=0, has_side_effects=True, vmem_limit_bytes=56 * 2**20
        ),
        name="relay",
    )(
        latents.reshape(GROUPS, rows, width),
        caption_kv[0, 0],
        caption_mask,
        query_weight.reshape(n_mp * CHUNKS, chunk, inner_width),
        out_weight[0],
        gate.reshape(n_mp * CHUNKS, 1, chunk),
        cotangent.reshape(GROUPS, rows, width),
    )
    tiles = heads // 2 if heads % 2 == 0 and half % (heads // 2 * 128) == 0 else 1
    part = inner_width // tiles
    band = pl.BlockSpec((GROUPS, rows, half // tiles), lambda i: (0, 0, i))
    section_out, input_grad, weight_grad = pl.pallas_call(
        result_kernel,
        grid=(tiles,),
        out_shape=(
            jax.ShapeDtypeStruct((GROUPS, rows, half), bf16),
            jax.ShapeDtypeStruct((GROUPS, rows, half), bf16),
            jax.ShapeDtypeStruct((inner_width, share), f32),
        ),
        in_specs=[
            pl.BlockSpec((n_dp, total_rows, part), lambda i: (0, 0, i)),
            pl.BlockSpec((n_dp, total_rows, share), lambda i: (0, 0, 0)),
            band,
            band,
        ],
        out_specs=(band, band, pl.BlockSpec((part, share), lambda i: (i, 0))),
        compiler_params=pltpu.CompilerParams(vmem_limit_bytes=56 * 2**20),
        name="results",
    )(attended, dproj, section_out, input_grad)
    shape = (1, 1, micro, tok, half)
    return (section_out.reshape(shape), input_grad.reshape(shape), weight_grad[None])


def solution(mesh):
    return jax.shard_map(
        per_device,
        mesh=mesh,
        in_specs=(
            P("dp", None, None, None),
            P("dp", "pipe", None, None, "mp"),
            P("dp", None),
            P("pipe", None, "mp"),
            P("pipe", "mp", None),
            P("pipe", None),
            P("dp", None, None, None),
        ),
        out_specs=(
            P("pipe", "dp", None, None, "mp"),
            P("pipe", "dp", None, None, "mp"),
            P("pipe", "mp", "dp"),
        ),
        check_vma=False,
    )
```

```python
import functools
import math

import jax
import jax.numpy as jnp
from jax import lax
from jax.experimental import pallas as pl
from jax.experimental.pallas import tpu as pltpu
from jax.sharding import PartitionSpec as P

HEAD_DIM = 128
GROUPS = 2
CHUNKS = 2
MESH = pl.DeviceIdType.MESH
NT = (((1,), (1,)), ((), ()))
TN = (((0,), (0,)), ((), ()))


def dot(a, b, dims=(((1,), (0,)), ((), ()))):
    return lax.dot_general(a, b, dims, preferred_element_type=jnp.float32)


def relay_kernel(
    sizes,
    tiles,
    lat,
    kv_any,
    mask,
    wq_any,
    wo_any,
    gate,
    cot,
    out_ref,
    dx_ref,
    wg_ref,
    att_all,
    dcol,
    wg_vmem,
    wqt,
    wot,
    kv,
    wq,
    wo,
    xbuf,
    dybuf,
    xsend,
    dxsend,
    psend,
    precv,
    bsend,
    brecv,
    own,
    prob_buf,
    qbuf,
    rbuf,
    dqbuf,
    pbuf,
    dpj,
    s_w,
    s_g,
    s_x,
    r_x,
    s_dy,
    r_dy,
    s_p,
    r_p,
    s_b,
    r_b,
    s_att,
    r_att,
    s_dp,
    r_dp,
):
    n_dp, n_pipe, n_mp = sizes
    groups, rows, width = lat.shape
    chunks, chunk = (xbuf.shape[2], xbuf.shape[4])
    inner_width = wo.shape[0]
    heads = inner_width // HEAD_DIM
    share = dpj.shape[2]
    slabs = chunk // share
    scale = 1.0 / math.sqrt(HEAD_DIM)
    z = lax.axis_index("dp")
    p = lax.axis_index("pipe")
    y = lax.axis_index("mp")
    first = p == 0
    last = p == n_pipe - 1

    def load(i, src, dst):
        return pltpu.make_async_copy(src, dst, s_w.at[i])

    load_wq = load(0, wq_any, wq)
    load_kv = load(1, kv_any, kv)
    load_wo = load(2, wo_any, wo)

    def load_rows(src, dst, sems):
        for m in range(groups):
            for c in range(chunks):
                for h in range(n_mp):
                    begin = (h * chunks + c) * chunk
                    pltpu.make_async_copy(
                        src.at[m, :, pl.ds(begin, chunk)], dst.at[m, h, c], sems.at[m, h, c]
                    ).start()

    @pl.when(first)
    def _():
        load_rows(lat, xbuf, r_x)

    load_wq.start()
    load_kv.start()
    load_wo.start()

    @pl.when(last)
    def _():
        load_rows(cot, dybuf, r_dy)

    barrier = pltpu.get_barrier_semaphore()

    def greet(target):
        pl.semaphore_signal(barrier, inc=1, device_id=target, device_id_type=MESH)

    for o in range(1, n_mp):
        greet({"mp": lax.rem(y + o, n_mp)})

    @pl.loop(1, n_dp)
    def _(k):
        greet({"dp": lax.rem(z + k, n_dp)})

    @pl.when(jnp.logical_not(first))
    def _():
        for h in range(n_mp):
            greet({"pipe": p - 1, "mp": h})

    @pl.when(jnp.logical_not(last))
    def _():
        for h in range(n_mp):
            greet({"pipe": p + 1, "mp": h})

    edges = first.astype(jnp.int32) + last.astype(jnp.int32)
    pl.semaphore_wait(barrier, (n_mp - 1) + (n_dp - 1) + n_mp * (2 - edges))

    def group_rows(m):
        return pl.ds(pl.multiple_of(m * rows, rows), rows)

    def columns(j):
        return pl.ds(pl.multiple_of(j * chunk, 128), chunk)

    def relay_copy(src, dst, send, recv, m, c, h, target, slot):
        return pltpu.make_async_remote_copy(
            src_ref=src.at[m, c],
            dst_ref=dst.at[m, h, c],
            send_sem=send.at[m, c, slot],
            recv_sem=recv.at[m, h, c],
            device_id=target,
            device_id_type=MESH,
        )

    def forward_copy(m, c, o):
        target = {"pipe": p + 1, "mp": lax.rem(y + o, n_mp)}
        return relay_copy(xsend, xbuf, s_x, r_x, m, c, y, target, o)

    def backward_copy(m, c, o):
        target = {"pipe": p - 1, "mp": lax.rem(y + o, n_mp)}
        return relay_copy(dxsend, dybuf, s_dy, r_dy, m, c, y, target, o)

    def share_copy(src, dst, send, recv, m, c, o):
        return pltpu.make_async_remote_copy(
            src_ref=src.at[m, o - 1, c],
            dst_ref=dst.at[m, o - 1, c],
            send_sem=send.at[m, o - 1, c],
            recv_sem=recv.at[m, o - 1, c],
            device_id={"mp": lax.rem(y + o, n_mp)},
            device_id_type=MESH,
        )

    def att_copy(m, k, source):
        piece = att_all.at[source, group_rows(m)]
        return pltpu.make_async_remote_copy(
            src_ref=piece,
            dst_ref=piece,
            send_sem=s_att.at[m, k],
            recv_sem=r_att.at[m, k],
            device_id={"dp": lax.rem(z + k, n_dp)},
            device_id_type=MESH,
        )

    def dproj_copy(m, k, source, owner):
        return pltpu.make_async_remote_copy(
            src_ref=dpj.at[owner, group_rows(m)],
            dst_ref=dcol.at[source, group_rows(m)],
            send_sem=s_dp.at[m, k],
            recv_sem=r_dp.at[m, k],
            device_id={"dp": lax.rem(z + k, n_dp)},
            device_id_type=MESH,
        )

    def head(t):
        return slice(t * HEAD_DIM, (t + 1) * HEAD_DIM)

    def fold(values):
        pieces = [values[:, i : i + 128] for i in range(0, values.shape[1], 128)]
        return functools.reduce(jnp.add, pieces)

    order = [(c, o) for c in range(chunks) for o in range(n_mp)]

    def forward_query(m):
        query_raw = jnp.zeros((rows, inner_width), jnp.float32)
        squares = jnp.zeros((rows, 128), jnp.float32)
        for c, o in order:
            h = lax.rem(y + o, n_mp)
            relay_copy(xsend, xbuf, s_x, r_x, m, c, h, {"mp": y}, 0).wait_recv()
            x = xbuf[m, h, c]
            query_raw += dot(x, wq[h * chunks + c])
            squares += fold(jnp.square(x.astype(jnp.float32)))
        squares = jnp.sum(squares, axis=-1, keepdims=True)
        scale_r = lax.rsqrt(squares / width + 1e-06)
        query = (query_raw * scale_r).astype(jnp.bfloat16)
        rbuf[m] = jnp.broadcast_to(scale_r, rbuf.shape[1:])
        qbuf[m] = query
        live = mask[...] > 0
        scores = jnp.stack([dot(query[:, head(t)], kv[0, :, head(t)], NT) for t in range(heads)])
        scores = jnp.where(live[None], scores * scale, -1e30)
        powers = jnp.exp(scores - jnp.max(scores, axis=-1, keepdims=True))
        prob = powers * (1.0 / jnp.sum(powers, axis=-1, keepdims=True))
        prob_buf[m] = prob
        probs = prob.astype(jnp.bfloat16)
        parts = [dot(probs[t], kv[1, :, head(t)]).astype(jnp.bfloat16) for t in range(heads)]
        att_all[z, group_rows(m)] = jnp.concatenate(parts, axis=1)

    def forward_share(m):
        attended = att_all[z, group_rows(m)]
        for o in range(1, n_mp):
            h = lax.rem(y + o, n_mp)
            for c in range(chunks):
                piece = dot(attended, wo[:, columns(h * chunks + c)])
                psend[m, o - 1, c] = piece.astype(jnp.bfloat16)
                share_copy(psend, precv, s_p, r_p, m, c, o).start()
        for c in range(chunks):
            own[0, m, c] = dot(attended, wo[:, columns(y * chunks + c)])

        @pl.loop(1, n_dp)
        def _(k):
            att_copy(m, k, z).start()

    def forward_finish(m):
        for c in range(chunks):
            total = own[0, m, c]
            for o in range(1, n_mp):
                share_copy(psend, precv, s_p, r_p, m, c, o).wait_recv()
                total += precv[m, o - 1, c].astype(jnp.float32)
            x_float = xbuf[m, y, c].astype(jnp.float32)
            result = (x_float + gate[y * chunks + c] * total).astype(jnp.bfloat16)
            xsend[m, c] = result

            @pl.when(jnp.logical_not(last))
            def _():
                for o in reversed(range(n_mp)):
                    forward_copy(m, c, o).start()

            out_ref[m, :, c * chunk : (c + 1) * chunk] = result

    def backward_query(m):
        d_att = jnp.zeros((rows, inner_width), jnp.float32)
        for c, o in order:
            h = lax.rem(y + o, n_mp)
            j = h * chunks + c

            relay_copy(dxsend, dybuf, s_dy, r_dy, m, c, h, {"mp": y}, 0).wait_recv()
            dproj = (gate[j] * dybuf[m, h, c].astype(jnp.float32)).astype(jnp.bfloat16)
            for t in range(slabs):
                dpj[j * slabs + t, group_rows(m)] = dproj[:, t * share : (t + 1) * share]
            d_att += dot(dproj, wot[j])

        d_att = d_att.astype(jnp.bfloat16)
        prob = prob_buf[m]
        d_prob = jnp.stack([dot(d_att[:, head(t)], kv[1, :, head(t)], NT) for t in range(heads)])
        mean = jnp.sum(prob * d_prob, axis=-1, keepdims=True)
        d_score = (prob * (d_prob - mean)).astype(jnp.bfloat16)
        parts = [dot(d_score[t], kv[0, :, head(t)]) for t in range(heads)]
        d_query = (jnp.concatenate(parts, axis=1) * scale).astype(jnp.bfloat16)
        dqbuf[m] = d_query
        both = d_query.astype(jnp.float32) * qbuf[m].astype(jnp.float32)
        inner = jnp.sum(fold(both), axis=-1, keepdims=True)
        pbuf[m] = jnp.broadcast_to(rbuf[m][:, :1] * inner / width, pbuf.shape[1:])

    def backward_share(m):
        d_query = dqbuf[m]
        pull = pbuf[m][:, :1]

        def piece_of(h, c):
            x_float = xbuf[m, h, c].astype(jnp.float32)
            return dot(d_query, wqt[h * chunks + c]) - x_float * pull

        for o in range(1, n_mp):
            h = lax.rem(y + o, n_mp)
            for c in range(chunks):
                bsend[m, o - 1, c] = piece_of(h, c).astype(jnp.bfloat16)
                share_copy(bsend, brecv, s_b, r_b, m, c, o).start()
        for c in range(chunks):
            own[1, m, c] = piece_of(y, c)

        @pl.loop(1, n_dp)
        def _(k):
            dproj_copy(m, k, z, lax.rem(z + k, n_dp)).start()

    def backward_finish(m):
        scale_r = rbuf[m][:, :1]
        for c in range(chunks):
            total = own[1, m, c]
            for o in range(1, n_mp):
                share_copy(bsend, brecv, s_b, r_b, m, c, o).wait_recv()
                total += brecv[m, o - 1, c].astype(jnp.float32)
            dy = dybuf[m, y, c].astype(jnp.float32)
            result = (dy + scale_r * total).astype(jnp.bfloat16)
            dxsend[m, c] = result

            @pl.when(jnp.logical_not(first))
            def _():
                for o in reversed(range(n_mp)):
                    backward_copy(m, c, o).start()

            dx_ref[m, :, c * chunk : (c + 1) * chunk] = result

    late = last.astype(jnp.int32)
    turn = groups * (1 - late)
    held_back = (groups + 1) * late

    def turn_weights():
        @pl.loop(0, n_mp * chunks)
        def _(j):
            wqt[j] = wq[j].T
            wot[j] = wo[:, columns(j)].T

    def weight_grad():
        dcol[z] = dpj[z]

        @pl.loop(0, groups)
        def _(m):
            @pl.loop(1, n_dp)
            def _(k):
                source = lax.rem(z + n_dp - k, n_dp)
                att_copy(m, k, source).wait_recv()
                dproj_copy(m, k, source, z).wait_recv()

        depth = n_dp * groups * rows
        right = dcol[...].reshape(depth, share)
        for i in range(tiles):
            cut = slice(i * (inner_width // tiles), (i + 1) * (inner_width // tiles))
            left = att_all[:, :, cut].reshape(depth, inner_width // tiles)
            wg_vmem[cut, :] = dot(left, right, TN)
            keep_grad(i).start()

    def keep_grad(i):
        cut = pl.ds(i * (inner_width // tiles), inner_width // tiles)
        return pltpu.make_async_copy(wg_vmem.at[cut], wg_ref.at[cut], s_g.at[i])

    load_wq.wait()
    load_kv.wait()

    @pl.loop(-1, 2 * groups + 3)
    def _(step):
        def phase(run, m):
            @pl.when(jnp.logical_and(m >= 0, m < groups))
            def _():
                run(m)

        phase(forward_query, step)

        @pl.when(step == jnp.where(first, 0, -1))
        def _():
            load_wo.wait()

        phase(forward_finish, step - held_back - 1)
        phase(forward_share, step - held_back)

        @pl.when(step == jnp.where(first, groups, -1))
        def _():
            turn_weights()

        phase(backward_query, step - turn)

        @pl.when(step == jnp.where(first, 2 * groups, 2 * groups + 2))
        def _():
            weight_grad()

        phase(backward_finish, step - turn - 1)
        phase(backward_share, step - turn)

    for i in range(tiles):
        keep_grad(i).wait()

    @pl.loop(0, groups)
    def _(m):
        @pl.loop(1, n_dp)
        def _(k):
            att_copy(m, k, z).wait_send()
            dproj_copy(m, k, z, lax.rem(z + k, n_dp)).wait_send()

        for c in range(chunks):
            for o in range(1, n_mp):
                share_copy(psend, precv, s_p, r_p, m, c, o).wait_send()
                share_copy(bsend, brecv, s_b, r_b, m, c, o).wait_send()

            @pl.when(jnp.logical_not(last))
            def _():
                for o in range(n_mp):
                    forward_copy(m, c, o).wait_send()

            @pl.when(jnp.logical_not(first))
            def _():
                for o in range(n_mp):
                    backward_copy(m, c, o).wait_send()


def result_kernel(out, dx, wg, out_ref, dx_ref, wg_ref):
    out_ref[...] = out[...]
    dx_ref[...] = dx[...]
    wg_ref[...] = wg[...]


def per_device(latents, caption_kv, caption_mask, query_weight, out_weight, gate, cotangent):
    micro, tok, width = latents.shape[1:]
    n_dp, n_pipe, n_mp = (lax.axis_size("dp"), lax.axis_size("pipe"), lax.axis_size("mp"))
    total_rows = micro * tok
    rows = total_rows // GROUPS
    half = width // n_mp
    chunk = half // CHUNKS
    inner_width = out_weight.shape[1]
    heads = inner_width // HEAD_DIM
    cap = caption_mask.shape[1]
    share = width // n_dp
    bf16, f32 = (jnp.bfloat16, jnp.float32)
    whole = (GROUPS, n_mp, CHUNKS, rows, chunk)
    mine = (GROUPS, CHUNKS, rows, chunk)
    cross = (GROUPS, n_mp - 1, CHUNKS, rows, chunk)
    sem = pltpu.SemaphoreType.DMA
    vmem = pl.BlockSpec(memory_space=pltpu.VMEM)
    tiles = heads // 2 if heads % 2 == 0 and half % (heads // 2 * 128) == 0 else 1
    part = inner_width // tiles
    anywhere = pl.BlockSpec(memory_space=pl.ANY)
    section_out, input_grad, weight_grad = pl.pallas_call(
        functools.partial(relay_kernel, (n_dp, n_pipe, n_mp), tiles),
        out_shape=(
            jax.ShapeDtypeStruct((GROUPS, rows, half), bf16),
            jax.ShapeDtypeStruct((GROUPS, rows, half), bf16),
            jax.ShapeDtypeStruct((inner_width, share), f32),
        ),
        in_specs=[anywhere, anywhere, vmem, anywhere, anywhere, vmem, anywhere],
        out_specs=(vmem, vmem, anywhere),
        scratch_shapes=[
            pltpu.VMEM((n_dp, total_rows, inner_width), bf16),
            pltpu.VMEM((n_dp, total_rows, share), bf16),
            pltpu.VMEM((inner_width, share), f32),
            pltpu.VMEM((n_mp * CHUNKS, inner_width, chunk), bf16),
            pltpu.VMEM((n_mp * CHUNKS, chunk, inner_width), bf16),
            pltpu.VMEM(caption_kv.shape[2:], bf16),
            pltpu.VMEM((n_mp * CHUNKS, chunk, inner_width), bf16),
            pltpu.VMEM(out_weight.shape[1:], bf16),
            pltpu.VMEM(whole, bf16),
            pltpu.VMEM(whole, bf16),
            pltpu.VMEM(mine, bf16),
            pltpu.VMEM(mine, bf16),
            pltpu.VMEM(cross, bf16),
            pltpu.VMEM(cross, bf16),
            pltpu.VMEM(cross, bf16),
            pltpu.VMEM(cross, bf16),
            pltpu.VMEM((2,) + mine, f32),
            pltpu.VMEM((GROUPS, heads, rows, cap), f32),
            pltpu.VMEM((GROUPS, rows, inner_width), bf16),
            pltpu.VMEM((GROUPS, rows, 128), f32),
            pltpu.VMEM((GROUPS, rows, inner_width), bf16),
            pltpu.VMEM((GROUPS, rows, 128), f32),
            pltpu.VMEM((n_dp, total_rows, share), bf16),
            sem((3,)),
            sem((tiles,)),
            sem((GROUPS, CHUNKS, n_mp)),
            sem((GROUPS, n_mp, CHUNKS)),
            sem((GROUPS, CHUNKS, n_mp)),
            sem((GROUPS, n_mp, CHUNKS)),
            sem((GROUPS, n_mp - 1, CHUNKS)),
            sem((GROUPS, n_mp - 1, CHUNKS)),
            sem((GROUPS, n_mp - 1, CHUNKS)),
            sem((GROUPS, n_mp - 1, CHUNKS)),
            sem((GROUPS, n_dp)),
            sem((GROUPS, n_dp)),
            sem((GROUPS, n_dp)),
            sem((GROUPS, n_dp)),
        ],
        compiler_params=pltpu.CompilerParams(
            collective_id=0, has_side_effects=True, vmem_limit_bytes=56 * 2**20
        ),
        name="relay",
    )(
        latents.reshape(GROUPS, rows, width),
        caption_kv[0, 0],
        caption_mask,
        query_weight.reshape(n_mp * CHUNKS, chunk, inner_width),
        out_weight[0],
        gate.reshape(n_mp * CHUNKS, 1, chunk),
        cotangent.reshape(GROUPS, rows, width),
    )
    band = pl.BlockSpec((GROUPS, rows, half // tiles), lambda i: (0, 0, i))
    grad_band = pl.BlockSpec((part, share), lambda i: (i, 0))
    section_out, input_grad, weight_grad = pl.pallas_call(
        result_kernel,
        grid=(tiles,),
        out_shape=(
            jax.ShapeDtypeStruct((GROUPS, rows, half), bf16),
            jax.ShapeDtypeStruct((GROUPS, rows, half), bf16),
            jax.ShapeDtypeStruct((inner_width, share), f32),
        ),
        in_specs=[band, band, grad_band],
        out_specs=(band, band, grad_band),
        compiler_params=pltpu.CompilerParams(vmem_limit_bytes=56 * 2**20),
        name="results",
    )(section_out, input_grad, weight_grad)
    shape = (1, 1, micro, tok, half)
    return (section_out.reshape(shape), input_grad.reshape(shape), weight_grad[None])


def solution(mesh):
    return jax.shard_map(
        per_device,
        mesh=mesh,
        in_specs=(
            P("dp", None, None, None),
            P("dp", "pipe", None, None, "mp"),
            P("dp", None),
            P("pipe", None, "mp"),
            P("pipe", "mp", None),
            P("pipe", None),
            P("dp", None, None, None),
        ),
        out_specs=(
            P("pipe", "dp", None, None, "mp"),
            P("pipe", "dp", None, None, "mp"),
            P("pipe", "mp", "dp"),
        ),
        check_vma=False,
    )
```

```python
import functools
import math

import jax
import jax.numpy as jnp
from jax import lax
from jax.experimental import pallas as pl
from jax.experimental.pallas import tpu as pltpu
from jax.sharding import PartitionSpec as P

HEAD_DIM = 128
GROUPS = 2
CHUNKS = 3
MESH = pl.DeviceIdType.MESH
NT = (((1,), (1,)), ((), ()))
TN = (((0,), (0,)), ((), ()))


def dot(a, b, dims=(((1,), (0,)), ((), ()))):
    return lax.dot_general(a, b, dims, preferred_element_type=jnp.float32)


def relay_kernel(
    sizes,
    tiles,
    lat,
    kv_any,
    mask,
    wq_any,
    wo_any,
    gate,
    cot,
    out_ref,
    dx_ref,
    wg_ref,
    att_all,
    dcol,
    att_t,
    wg_vmem,
    wqt,
    wot,
    kv,
    wq,
    wo,
    xbuf,
    dybuf,
    xsend,
    dxsend,
    psend,
    precv,
    bsend,
    brecv,
    own,
    prob_buf,
    qbuf,
    rbuf,
    dqbuf,
    pbuf,
    dpj,
    s_w,
    s_g,
    s_x,
    r_x,
    s_dy,
    r_dy,
    s_p,
    r_p,
    s_b,
    r_b,
    s_att,
    r_att,
    s_dp,
    r_dp,
):
    n_dp, n_pipe, n_mp = sizes
    groups, rows, width = lat.shape
    chunks, chunk = (xbuf.shape[2], xbuf.shape[4])
    inner_width = wo.shape[0]
    heads = inner_width // HEAD_DIM
    share = dpj.shape[2]
    unit = math.gcd(chunk, share)
    per_slab = share // unit
    depth = n_dp * groups * rows
    scale = 1.0 / math.sqrt(HEAD_DIM)
    z = lax.axis_index("dp")
    p = lax.axis_index("pipe")
    y = lax.axis_index("mp")
    first = p == 0
    last = p == n_pipe - 1

    def load(i, src, dst):
        return pltpu.make_async_copy(src, dst, s_w.at[i])

    load_wq = load(0, wq_any, wq)
    load_kv = load(1, kv_any, kv)
    load_wo = load(2, wo_any, wo)

    def load_rows(src, dst, sems):
        for m in range(groups):
            for c in range(chunks):
                for h in range(n_mp):
                    begin = (h * chunks + c) * chunk
                    pltpu.make_async_copy(
                        src.at[m, :, pl.ds(begin, chunk)], dst.at[m, h, c], sems.at[m, h, c]
                    ).start()

    @pl.when(first)
    def _():
        load_rows(lat, xbuf, r_x)

    load_wq.start()
    load_kv.start()
    load_wo.start()

    @pl.when(last)
    def _():
        load_rows(cot, dybuf, r_dy)

    barrier = pltpu.get_barrier_semaphore()

    def greet(target):
        pl.semaphore_signal(barrier, inc=1, device_id=target, device_id_type=MESH)

    for o in range(1, n_mp):
        greet({"mp": lax.rem(y + o, n_mp)})

    @pl.loop(1, n_dp)
    def _(k):
        greet({"dp": lax.rem(z + k, n_dp)})

    @pl.when(jnp.logical_not(first))
    def _():
        for h in range(n_mp):
            greet({"pipe": p - 1, "mp": h})

    @pl.when(jnp.logical_not(last))
    def _():
        for h in range(n_mp):
            greet({"pipe": p + 1, "mp": h})

    edges = first.astype(jnp.int32) + last.astype(jnp.int32)
    pl.semaphore_wait(barrier, (n_mp - 1) + (n_dp - 1) + n_mp * (2 - edges))

    def group_rows(m):
        return pl.ds(pl.multiple_of(m * rows, rows), rows)

    def columns(j):
        return pl.ds(pl.multiple_of(j * chunk, 128), chunk)

    def relay_copy(src, dst, send, recv, m, c, h, target, slot):
        return pltpu.make_async_remote_copy(
            src_ref=src.at[m, c],
            dst_ref=dst.at[m, h, c],
            send_sem=send.at[m, c, slot],
            recv_sem=recv.at[m, h, c],
            device_id=target,
            device_id_type=MESH,
        )

    def forward_copy(m, c, o):
        target = {"pipe": p + 1, "mp": lax.rem(y + o, n_mp)}
        return relay_copy(xsend, xbuf, s_x, r_x, m, c, y, target, o)

    def backward_copy(m, c, o):
        target = {"pipe": p - 1, "mp": lax.rem(y + o, n_mp)}
        return relay_copy(dxsend, dybuf, s_dy, r_dy, m, c, y, target, o)

    def share_copy(src, dst, send, recv, m, c, o):
        return pltpu.make_async_remote_copy(
            src_ref=src.at[m, o - 1, c],
            dst_ref=dst.at[m, o - 1, c],
            send_sem=send.at[m, o - 1, c],
            recv_sem=recv.at[m, o - 1, c],
            device_id={"mp": lax.rem(y + o, n_mp)},
            device_id_type=MESH,
        )

    def att_copy(m, k, source):
        piece = att_all.at[source, group_rows(m)]
        return pltpu.make_async_remote_copy(
            src_ref=piece,
            dst_ref=piece,
            send_sem=s_att.at[m, k],
            recv_sem=r_att.at[m, k],
            device_id={"dp": lax.rem(z + k, n_dp)},
            device_id_type=MESH,
        )

    def dproj_copy(m, k, source, owner):
        return pltpu.make_async_remote_copy(
            src_ref=dpj.at[owner, group_rows(m)],
            dst_ref=dcol.at[source, group_rows(m)],
            send_sem=s_dp.at[m, k],
            recv_sem=r_dp.at[m, k],
            device_id={"dp": lax.rem(z + k, n_dp)},
            device_id_type=MESH,
        )

    def head(t):
        return slice(t * HEAD_DIM, (t + 1) * HEAD_DIM)

    def fold(values):
        pieces = [values[:, i : i + 128] for i in range(0, values.shape[1], 128)]
        return functools.reduce(jnp.add, pieces)

    order = [(c, o) for c in range(chunks) for o in range(n_mp)]

    def forward_query(m):
        query_raw = jnp.zeros((rows, inner_width), jnp.float32)
        squares = jnp.zeros((rows, 128), jnp.float32)
        for c, o in order:
            h = lax.rem(y + o, n_mp)
            relay_copy(xsend, xbuf, s_x, r_x, m, c, h, {"mp": y}, 0).wait_recv()
            x = xbuf[m, h, c]
            query_raw += dot(x, wq[h * chunks + c])
            squares += fold(jnp.square(x.astype(jnp.float32)))
        squares = jnp.sum(squares, axis=-1, keepdims=True)
        scale_r = lax.rsqrt(squares / width + 1e-06)
        query = (query_raw * scale_r).astype(jnp.bfloat16)
        rbuf[m] = jnp.broadcast_to(scale_r, rbuf.shape[1:])
        qbuf[m] = query
        live = mask[...] > 0
        scores = jnp.stack([dot(query[:, head(t)], kv[0, :, head(t)], NT) for t in range(heads)])
        scores = jnp.where(live[None], scores * scale, -1e30)
        powers = jnp.exp(scores - jnp.max(scores, axis=-1, keepdims=True))
        prob = powers * (1.0 / jnp.sum(powers, axis=-1, keepdims=True))
        prob_buf[m] = prob
        probs = prob.astype(jnp.bfloat16)
        parts = [dot(probs[t], kv[1, :, head(t)]).astype(jnp.bfloat16) for t in range(heads)]
        att_all[z, group_rows(m)] = jnp.concatenate(parts, axis=1)

    def forward_share(m):
        attended = att_all[z, group_rows(m)]
        for o in range(1, n_mp):
            h = lax.rem(y + o, n_mp)
            for c in range(chunks):
                piece = dot(attended, wo[:, columns(h * chunks + c)])
                psend[m, o - 1, c] = piece.astype(jnp.bfloat16)
                share_copy(psend, precv, s_p, r_p, m, c, o).start()
        for c in range(chunks):
            own[0, m, c] = dot(attended, wo[:, columns(y * chunks + c)])

        @pl.loop(1, n_dp)
        def _(k):
            att_copy(m, k, z).start()

    def forward_finish(m):
        for c in range(chunks):
            total = own[0, m, c]
            for o in range(1, n_mp):
                share_copy(psend, precv, s_p, r_p, m, c, o).wait_recv()
                total += precv[m, o - 1, c].astype(jnp.float32)
            x_float = xbuf[m, y, c].astype(jnp.float32)
            result = (x_float + gate[y * chunks + c] * total).astype(jnp.bfloat16)
            xsend[m, c] = result

            @pl.when(jnp.logical_not(last))
            def _():
                for o in reversed(range(n_mp)):
                    forward_copy(m, c, o).start()

            out_ref[m, :, c * chunk : (c + 1) * chunk] = result

    def backward_query(m):
        d_att = jnp.zeros((rows, inner_width), jnp.float32)
        for c, o in order:
            h = lax.rem(y + o, n_mp)
            j = h * chunks + c

            relay_copy(dxsend, dybuf, s_dy, r_dy, m, c, h, {"mp": y}, 0).wait_recv()
            dproj = (gate[j] * dybuf[m, h, c].astype(jnp.float32)).astype(jnp.bfloat16)
            for t in range(chunk // unit):
                index = j * (chunk // unit) + t
                piece = dproj[:, t * unit : (t + 1) * unit]
                if per_slab == 1:
                    dpj[index, group_rows(m)] = piece
                else:
                    begin = pl.multiple_of(lax.rem(index, per_slab) * unit, unit)
                    dpj[lax.div(index, per_slab), group_rows(m), pl.ds(begin, unit)] = piece
            d_att += dot(dproj, wot[j])

        d_att = d_att.astype(jnp.bfloat16)
        prob = prob_buf[m]
        d_prob = jnp.stack([dot(d_att[:, head(t)], kv[1, :, head(t)], NT) for t in range(heads)])
        mean = jnp.sum(prob * d_prob, axis=-1, keepdims=True)
        d_score = (prob * (d_prob - mean)).astype(jnp.bfloat16)
        parts = [dot(d_score[t], kv[0, :, head(t)]) for t in range(heads)]
        d_query = (jnp.concatenate(parts, axis=1) * scale).astype(jnp.bfloat16)
        dqbuf[m] = d_query
        both = d_query.astype(jnp.float32) * qbuf[m].astype(jnp.float32)
        inner = jnp.sum(fold(both), axis=-1, keepdims=True)
        pbuf[m] = jnp.broadcast_to(rbuf[m][:, :1] * inner / width, pbuf.shape[1:])

    def backward_share(m):
        d_query = dqbuf[m]
        pull = pbuf[m][:, :1]

        def piece_of(h, c):
            x_float = xbuf[m, h, c].astype(jnp.float32)
            return dot(d_query, wqt[h * chunks + c]) - x_float * pull

        for o in range(1, n_mp):
            h = lax.rem(y + o, n_mp)
            for c in range(chunks):
                bsend[m, o - 1, c] = piece_of(h, c).astype(jnp.bfloat16)
                share_copy(bsend, brecv, s_b, r_b, m, c, o).start()
        for c in range(chunks):
            own[1, m, c] = piece_of(y, c)

        @pl.loop(1, n_dp)
        def _(k):
            dproj_copy(m, k, z, lax.rem(z + k, n_dp)).start()

    def backward_finish(m):
        scale_r = rbuf[m][:, :1]
        for c in range(chunks):
            total = own[1, m, c]
            for o in range(1, n_mp):
                share_copy(bsend, brecv, s_b, r_b, m, c, o).wait_recv()
                total += brecv[m, o - 1, c].astype(jnp.float32)
            dy = dybuf[m, y, c].astype(jnp.float32)
            result = (dy + scale_r * total).astype(jnp.bfloat16)
            dxsend[m, c] = result

            @pl.when(jnp.logical_not(first))
            def _():
                for o in reversed(range(n_mp)):
                    backward_copy(m, c, o).start()

            dx_ref[m, :, c * chunk : (c + 1) * chunk] = result

    late = last.astype(jnp.int32)
    turn = groups * (1 - late)
    held_back = (groups + 1) * late

    def turn_weights():
        @pl.loop(0, n_mp * chunks)
        def _(j):
            wqt[j] = wq[j].T
            wot[j] = wo[:, columns(j)].T

    def turn_attended():
        @pl.loop(0, groups)
        def _(m):
            @pl.loop(1, n_dp)
            def _(k):
                att_copy(m, k, lax.rem(z + n_dp - k, n_dp)).wait_recv()

        if depth <= 1024:
            att_t[...] = att_all[...].reshape(depth, inner_width).T

    def weight_grad():
        dcol[z] = dpj[z]

        @pl.loop(0, groups)
        def _(m):
            @pl.loop(1, n_dp)
            def _(k):
                dproj_copy(m, k, lax.rem(z + n_dp - k, n_dp), z).wait_recv()

        right = dcol[...].reshape(depth, share)
        for i in range(tiles):
            cut = slice(i * (inner_width // tiles), (i + 1) * (inner_width // tiles))
            if depth <= 1024:
                wg_vmem[cut, :] = dot(att_t[cut, :], right)
            else:
                left = att_all[:, :, cut].reshape(depth, inner_width // tiles)
                wg_vmem[cut, :] = dot(left, right, TN)
            keep_grad(i).start()

    def keep_grad(i):
        cut = pl.ds(i * (inner_width // tiles), inner_width // tiles)
        return pltpu.make_async_copy(wg_vmem.at[cut], wg_ref.at[cut], s_g.at[i])

    load_wq.wait()
    load_kv.wait()

    @pl.loop(-1, 2 * groups + 3)
    def _(step):
        def phase(run, m):
            @pl.when(jnp.logical_and(m >= 0, m < groups))
            def _():
                run(m)

        phase(forward_query, step)

        @pl.when(step == jnp.where(first, 0, -1))
        def _():
            load_wo.wait()

        phase(forward_finish, step - held_back - 1)
        phase(forward_share, step - held_back)

        @pl.when(step == jnp.where(first, groups, -1))
        def _():
            turn_weights()

        @pl.when(step == jnp.where(first, groups, 2 * groups + 2))
        def _():
            turn_attended()

        phase(backward_query, step - turn)

        @pl.when(step == jnp.where(first, 2 * groups, 2 * groups + 2))
        def _():
            weight_grad()

        phase(backward_finish, step - turn - 1)
        phase(backward_share, step - turn)

    for i in range(tiles):
        keep_grad(i).wait()

    @pl.loop(0, groups)
    def _(m):
        @pl.loop(1, n_dp)
        def _(k):
            att_copy(m, k, z).wait_send()
            dproj_copy(m, k, z, lax.rem(z + k, n_dp)).wait_send()

        for c in range(chunks):
            for o in range(1, n_mp):
                share_copy(psend, precv, s_p, r_p, m, c, o).wait_send()
                share_copy(bsend, brecv, s_b, r_b, m, c, o).wait_send()

            @pl.when(jnp.logical_not(last))
            def _():
                for o in range(n_mp):
                    forward_copy(m, c, o).wait_send()

            @pl.when(jnp.logical_not(first))
            def _():
                for o in range(n_mp):
                    backward_copy(m, c, o).wait_send()


def result_kernel(out, dx, wg, out_ref, dx_ref, wg_ref, sems):
    parts = sems.shape[0] - 2
    size = wg.shape[0] // parts
    copies = [
        pltpu.make_async_copy(wg.at[pl.ds(i * size, size)], wg_ref.at[pl.ds(i * size, size)], sems.at[i])
        for i in range(parts)
    ]
    copies.append(pltpu.make_async_copy(out, out_ref, sems.at[parts]))
    copies.append(pltpu.make_async_copy(dx, dx_ref, sems.at[parts + 1]))
    for copy in copies:
        copy.start()
    for copy in copies:
        copy.wait()


def per_device(latents, caption_kv, caption_mask, query_weight, out_weight, gate, cotangent):
    micro, tok, width = latents.shape[1:]
    n_dp, n_pipe, n_mp = (lax.axis_size("dp"), lax.axis_size("pipe"), lax.axis_size("mp"))
    total_rows = micro * tok
    rows = total_rows // GROUPS
    half = width // n_mp
    chunk = half // CHUNKS
    inner_width = out_weight.shape[1]
    heads = inner_width // HEAD_DIM
    cap = caption_mask.shape[1]
    share = width // n_dp
    bf16, f32 = (jnp.bfloat16, jnp.float32)
    whole = (GROUPS, n_mp, CHUNKS, rows, chunk)
    mine = (GROUPS, CHUNKS, rows, chunk)
    cross = (GROUPS, n_mp - 1, CHUNKS, rows, chunk)
    sem = pltpu.SemaphoreType.DMA
    vmem = pl.BlockSpec(memory_space=pltpu.VMEM)
    tiles = heads // 2 if heads % 2 == 0 and half % (heads // 2 * 128) == 0 else 1
    anywhere = pl.BlockSpec(memory_space=pl.ANY)
    section_out, input_grad, weight_grad = pl.pallas_call(
        functools.partial(relay_kernel, (n_dp, n_pipe, n_mp), tiles),
        out_shape=(
            jax.ShapeDtypeStruct((GROUPS, rows, half), bf16),
            jax.ShapeDtypeStruct((GROUPS, rows, half), bf16),
            jax.ShapeDtypeStruct((inner_width, share), f32),
        ),
        in_specs=[anywhere, anywhere, vmem, anywhere, anywhere, vmem, anywhere],
        out_specs=(vmem, vmem, anywhere),
        scratch_shapes=[
            pltpu.VMEM((n_dp, total_rows, inner_width), bf16),
            pltpu.VMEM((n_dp, total_rows, share), bf16),
            pltpu.VMEM((inner_width, min(n_dp * total_rows, 1024)), bf16),
            pltpu.VMEM((inner_width, share), f32),
            pltpu.VMEM((n_mp * CHUNKS, inner_width, chunk), bf16),
            pltpu.VMEM((n_mp * CHUNKS, chunk, inner_width), bf16),
            pltpu.VMEM(caption_kv.shape[2:], bf16),
            pltpu.VMEM((n_mp * CHUNKS, chunk, inner_width), bf16),
            pltpu.VMEM(out_weight.shape[1:], bf16),
            pltpu.VMEM(whole, bf16),
            pltpu.VMEM(whole, bf16),
            pltpu.VMEM(mine, bf16),
            pltpu.VMEM(mine, bf16),
            pltpu.VMEM(cross, bf16),
            pltpu.VMEM(cross, bf16),
            pltpu.VMEM(cross, bf16),
            pltpu.VMEM(cross, bf16),
            pltpu.VMEM((2,) + mine, f32),
            pltpu.VMEM((GROUPS, heads, rows, cap), f32),
            pltpu.VMEM((GROUPS, rows, inner_width), bf16),
            pltpu.VMEM((GROUPS, rows, 128), f32),
            pltpu.VMEM((GROUPS, rows, inner_width), bf16),
            pltpu.VMEM((GROUPS, rows, 128), f32),
            pltpu.VMEM((n_dp, total_rows, share), bf16),
            sem((3,)),
            sem((tiles,)),
            sem((GROUPS, CHUNKS, n_mp)),
            sem((GROUPS, n_mp, CHUNKS)),
            sem((GROUPS, CHUNKS, n_mp)),
            sem((GROUPS, n_mp, CHUNKS)),
            sem((GROUPS, n_mp - 1, CHUNKS)),
            sem((GROUPS, n_mp - 1, CHUNKS)),
            sem((GROUPS, n_mp - 1, CHUNKS)),
            sem((GROUPS, n_mp - 1, CHUNKS)),
            sem((GROUPS, n_dp)),
            sem((GROUPS, n_dp)),
            sem((GROUPS, n_dp)),
            sem((GROUPS, n_dp)),
        ],
        compiler_params=pltpu.CompilerParams(
            collective_id=0, has_side_effects=True, vmem_limit_bytes=56 * 2**20
        ),
        name="relay",
    )(
        latents.reshape(GROUPS, rows, width),
        caption_kv[0, 0],
        caption_mask,
        query_weight.reshape(n_mp * CHUNKS, chunk, inner_width),
        out_weight[0],
        gate.reshape(n_mp * CHUNKS, 1, chunk),
        cotangent.reshape(GROUPS, rows, width),
    )
    section_out, input_grad, weight_grad = pl.pallas_call(
        result_kernel,
        out_shape=(
            jax.ShapeDtypeStruct((GROUPS, rows, half), bf16),
            jax.ShapeDtypeStruct((GROUPS, rows, half), bf16),
            jax.ShapeDtypeStruct((inner_width, share), f32),
        ),
        in_specs=[anywhere] * 3,
        out_specs=(anywhere,) * 3,
        scratch_shapes=[sem((2 * tiles + 2,))],
        compiler_params=pltpu.CompilerParams(vmem_limit_bytes=56 * 2**20),
        name="results",
    )(section_out, input_grad, weight_grad)
    shape = (1, 1, micro, tok, half)
    return (section_out.reshape(shape), input_grad.reshape(shape), weight_grad[None])


def solution(mesh):
    return jax.shard_map(
        per_device,
        mesh=mesh,
        in_specs=(
            P("dp", None, None, None),
            P("dp", "pipe", None, None, "mp"),
            P("dp", None),
            P("pipe", None, "mp"),
            P("pipe", "mp", None),
            P("pipe", None),
            P("dp", None, None, None),
        ),
        out_specs=(
            P("pipe", "dp", None, None, "mp"),
            P("pipe", "dp", None, None, "mp"),
            P("pipe", "mp", "dp"),
        ),
        check_vma=False,
    )
```

```python
import functools
import math

import jax
import jax.numpy as jnp
from jax import lax
from jax.experimental import pallas as pl
from jax.experimental.pallas import tpu as pltpu
from jax.sharding import PartitionSpec as P

HEAD_DIM = 128
GROUPS = 2
CHUNKS = 3
MESH = pl.DeviceIdType.MESH
NT = (((1,), (1,)), ((), ()))
TN = (((0,), (0,)), ((), ()))


def dot(a, b, dims=(((1,), (0,)), ((), ()))):
    return lax.dot_general(a, b, dims, preferred_element_type=jnp.float32)


def relay_kernel(
    sizes,
    tiles,
    lat,
    kv_any,
    mask,
    wq_any,
    wo_any,
    gate,
    cot,
    out_ref,
    dx_ref,
    wg_ref,
    att_all,
    dcol,
    att_t,
    wg_vmem,
    wqt,
    wot,
    kv,
    wq,
    wo,
    xbuf,
    dybuf,
    xsend,
    dxsend,
    psend,
    precv,
    bsend,
    brecv,
    own,
    prob_buf,
    qbuf,
    rbuf,
    dqbuf,
    pbuf,
    dpj,
    s_w,
    s_g,
    s_x,
    r_x,
    s_dy,
    r_dy,
    s_p,
    r_p,
    s_b,
    r_b,
    s_att,
    r_att,
    s_dp,
    r_dp,
):
    n_dp, n_pipe, n_mp = sizes
    groups, rows, width = lat.shape
    chunks, chunk = (xbuf.shape[2], xbuf.shape[4])
    inner_width = wo.shape[0]
    heads = inner_width // HEAD_DIM
    share = dpj.shape[2]
    unit = math.gcd(chunk, share)
    per_slab = share // unit
    depth = n_dp * groups * rows
    scale = 1.0 / math.sqrt(HEAD_DIM)
    z = lax.axis_index("dp")
    p = lax.axis_index("pipe")
    y = lax.axis_index("mp")
    first = p == 0
    last = p == n_pipe - 1

    def load(i, src, dst):
        return pltpu.make_async_copy(src, dst, s_w.at[i])

    def load_wq(j):
        return load(2 + j, wq_any.at[j], wq.at[j])

    load_kv = load(0, kv_any, kv)
    load_wo = load(1, wo_any, wo)

    def load_rows(src, dst, sems):
        for m in range(groups):
            for c in range(chunks):
                for h in range(n_mp):
                    begin = (h * chunks + c) * chunk
                    pltpu.make_async_copy(
                        src.at[m, :, pl.ds(begin, chunk)], dst.at[m, h, c], sems.at[m, h, c]
                    ).start()

    @pl.when(first)
    def _():
        load_rows(lat, xbuf, r_x)

    load_kv.start()
    for c in range(chunks):
        for h in range(n_mp):
            load_wq(h * chunks + c).start()
    load_wo.start()

    @pl.when(last)
    def _():
        load_rows(cot, dybuf, r_dy)

    barrier = pltpu.get_barrier_semaphore()

    def greet(target):
        pl.semaphore_signal(barrier, inc=1, device_id=target, device_id_type=MESH)

    for o in range(1, n_mp):
        greet({"mp": lax.rem(y + o, n_mp)})

    @pl.loop(1, n_dp)
    def _(k):
        greet({"dp": lax.rem(z + k, n_dp)})

    @pl.when(jnp.logical_not(first))
    def _():
        for h in range(n_mp):
            greet({"pipe": p - 1, "mp": h})

    @pl.when(jnp.logical_not(last))
    def _():
        for h in range(n_mp):
            greet({"pipe": p + 1, "mp": h})

    edges = first.astype(jnp.int32) + last.astype(jnp.int32)
    pl.semaphore_wait(barrier, (n_mp - 1) + (n_dp - 1) + n_mp * (2 - edges))

    def group_rows(m):
        return pl.ds(pl.multiple_of(m * rows, rows), rows)

    def columns(j):
        return pl.ds(pl.multiple_of(j * chunk, 128), chunk)

    def relay_copy(src, dst, send, recv, m, c, h, target, slot):
        return pltpu.make_async_remote_copy(
            src_ref=src.at[m, c],
            dst_ref=dst.at[m, h, c],
            send_sem=send.at[m, c, slot],
            recv_sem=recv.at[m, h, c],
            device_id=target,
            device_id_type=MESH,
        )

    def forward_copy(m, c, o):
        target = {"pipe": p + 1, "mp": lax.rem(y + o, n_mp)}
        return relay_copy(xsend, xbuf, s_x, r_x, m, c, y, target, o)

    def backward_copy(m, c, o):
        target = {"pipe": p - 1, "mp": lax.rem(y + o, n_mp)}
        return relay_copy(dxsend, dybuf, s_dy, r_dy, m, c, y, target, o)

    def share_copy(src, dst, send, recv, m, c, o):
        return pltpu.make_async_remote_copy(
            src_ref=src.at[m, o - 1, c],
            dst_ref=dst.at[m, o - 1, c],
            send_sem=send.at[m, o - 1, c],
            recv_sem=recv.at[m, o - 1, c],
            device_id={"mp": lax.rem(y + o, n_mp)},
            device_id_type=MESH,
        )

    def att_copy(m, k, source):
        piece = att_all.at[source, group_rows(m)]
        return pltpu.make_async_remote_copy(
            src_ref=piece,
            dst_ref=piece,
            send_sem=s_att.at[m, k],
            recv_sem=r_att.at[m, k],
            device_id={"dp": lax.rem(z + k, n_dp)},
            device_id_type=MESH,
        )

    def dproj_copy(m, k, source, owner):
        return pltpu.make_async_remote_copy(
            src_ref=dpj.at[owner, group_rows(m)],
            dst_ref=dcol.at[source, group_rows(m)],
            send_sem=s_dp.at[m, k],
            recv_sem=r_dp.at[m, k],
            device_id={"dp": lax.rem(z + k, n_dp)},
            device_id_type=MESH,
        )

    def head(t):
        return slice(t * HEAD_DIM, (t + 1) * HEAD_DIM)

    def fold(values):
        pieces = [values[:, i : i + 128] for i in range(0, values.shape[1], 128)]
        return functools.reduce(jnp.add, pieces)

    order = [(c, o) for c in range(chunks) for o in range(n_mp)]

    def forward_query(m):
        query_raw = jnp.zeros((rows, inner_width), jnp.float32)
        squares = jnp.zeros((rows, 128), jnp.float32)
        for c, o in order:
            h = lax.rem(y + o, n_mp)
            if o == 0:
                for g in range(n_mp):
                    relay_copy(xsend, xbuf, s_x, r_x, m, c, g, {"mp": y}, 0).wait_recv()

                @pl.when(jnp.logical_and(first, m == 0))
                def _():
                    for g in range(n_mp):
                        load_wq(g * chunks + c).wait()

            x = xbuf[m, h, c]
            query_raw += dot(x, wq[h * chunks + c])
            squares += fold(jnp.square(x.astype(jnp.float32)))
        squares = jnp.sum(squares, axis=-1, keepdims=True)
        scale_r = lax.rsqrt(squares / width + 1e-06)
        query = (query_raw * scale_r).astype(jnp.bfloat16)
        rbuf[m] = jnp.broadcast_to(scale_r, rbuf.shape[1:])
        qbuf[m] = query
        live = mask[...] > 0
        scores = jnp.stack([dot(query[:, head(t)], kv[0, :, head(t)], NT) for t in range(heads)])
        scores = jnp.where(live[None], scores * scale, -1e30)
        powers = jnp.exp(scores - jnp.max(scores, axis=-1, keepdims=True))
        prob = powers * (1.0 / jnp.sum(powers, axis=-1, keepdims=True))
        prob_buf[m] = prob
        probs = prob.astype(jnp.bfloat16)
        parts = [dot(probs[t], kv[1, :, head(t)]).astype(jnp.bfloat16) for t in range(heads)]
        att_all[z, group_rows(m)] = jnp.concatenate(parts, axis=1)

    def forward_share(m):
        attended = att_all[z, group_rows(m)]
        for o in range(1, n_mp):
            h = lax.rem(y + o, n_mp)
            for c in range(chunks):
                piece = dot(attended, wo[:, columns(h * chunks + c)])
                psend[m, o - 1, c] = piece.astype(jnp.bfloat16)
                share_copy(psend, precv, s_p, r_p, m, c, o).start()
        for c in range(chunks):
            own[0, m, c] = dot(attended, wo[:, columns(y * chunks + c)])

        @pl.loop(1, n_dp)
        def _(k):
            att_copy(m, k, z).start()

    def forward_finish(m):
        for c in range(chunks):
            total = own[0, m, c]
            for o in range(1, n_mp):
                share_copy(psend, precv, s_p, r_p, m, c, o).wait_recv()
                total += precv[m, o - 1, c].astype(jnp.float32)
            x_float = xbuf[m, y, c].astype(jnp.float32)
            result = (x_float + gate[y * chunks + c] * total).astype(jnp.bfloat16)
            xsend[m, c] = result

            @pl.when(jnp.logical_not(last))
            def _():
                for o in reversed(range(n_mp)):
                    forward_copy(m, c, o).start()

            out_ref[m, :, c * chunk : (c + 1) * chunk] = result

    def backward_query(m):
        d_att = jnp.zeros((rows, inner_width), jnp.float32)
        for c, o in order:
            h = lax.rem(y + o, n_mp)
            j = h * chunks + c

            if o == 0:
                for g in range(n_mp):
                    relay_copy(dxsend, dybuf, s_dy, r_dy, m, c, g, {"mp": y}, 0).wait_recv()

            dproj = (gate[j] * dybuf[m, h, c].astype(jnp.float32)).astype(jnp.bfloat16)
            for t in range(chunk // unit):
                index = j * (chunk // unit) + t
                piece = dproj[:, t * unit : (t + 1) * unit]
                if per_slab == 1:
                    dpj[index, group_rows(m)] = piece
                else:
                    begin = pl.multiple_of(lax.rem(index, per_slab) * unit, unit)
                    dpj[lax.div(index, per_slab), group_rows(m), pl.ds(begin, unit)] = piece
            d_att += dot(dproj, wot[j])

        d_att = d_att.astype(jnp.bfloat16)
        prob = prob_buf[m]
        d_prob = jnp.stack([dot(d_att[:, head(t)], kv[1, :, head(t)], NT) for t in range(heads)])
        mean = jnp.sum(prob * d_prob, axis=-1, keepdims=True)
        d_score = (prob * (d_prob - mean)).astype(jnp.bfloat16)
        parts = [dot(d_score[t], kv[0, :, head(t)]) for t in range(heads)]
        d_query = (jnp.concatenate(parts, axis=1) * scale).astype(jnp.bfloat16)
        dqbuf[m] = d_query
        both = d_query.astype(jnp.float32) * qbuf[m].astype(jnp.float32)
        inner = jnp.sum(fold(both), axis=-1, keepdims=True)
        pbuf[m] = jnp.broadcast_to(rbuf[m][:, :1] * inner / width, pbuf.shape[1:])

    def backward_share(m):
        d_query = dqbuf[m]
        pull = pbuf[m][:, :1]

        def piece_of(h, c):
            x_float = xbuf[m, h, c].astype(jnp.float32)
            return dot(d_query, wqt[h * chunks + c]) - x_float * pull

        for o in range(1, n_mp):
            h = lax.rem(y + o, n_mp)
            for c in range(chunks):
                bsend[m, o - 1, c] = piece_of(h, c).astype(jnp.bfloat16)
                share_copy(bsend, brecv, s_b, r_b, m, c, o).start()
        for c in range(chunks):
            own[1, m, c] = piece_of(y, c)

        @pl.loop(1, n_dp)
        def _(k):
            dproj_copy(m, k, z, lax.rem(z + k, n_dp)).start()

    def backward_finish(m):
        scale_r = rbuf[m][:, :1]
        for c in range(chunks):
            total = own[1, m, c]
            for o in range(1, n_mp):
                share_copy(bsend, brecv, s_b, r_b, m, c, o).wait_recv()
                total += brecv[m, o - 1, c].astype(jnp.float32)
            dy = dybuf[m, y, c].astype(jnp.float32)
            result = (dy + scale_r * total).astype(jnp.bfloat16)
            dxsend[m, c] = result

            @pl.when(jnp.logical_not(first))
            def _():
                for o in reversed(range(n_mp)):
                    backward_copy(m, c, o).start()

            dx_ref[m, :, c * chunk : (c + 1) * chunk] = result

    late = last.astype(jnp.int32)
    turn = groups * (1 - late)
    held_back = (groups + 1) * late

    def turn_weights():
        @pl.loop(0, n_mp * chunks)
        def _(j):
            wqt[j] = wq[j].T
            wot[j] = wo[:, columns(j)].T

    def turn_attended():
        @pl.loop(0, groups)
        def _(m):
            @pl.loop(1, n_dp)
            def _(k):
                att_copy(m, k, lax.rem(z + n_dp - k, n_dp)).wait_recv()

        if depth <= 1024:
            att_t[...] = att_all[...].reshape(depth, inner_width).T

    def weight_grad():
        dcol[z] = dpj[z]

        @pl.loop(0, groups)
        def _(m):
            @pl.loop(1, n_dp)
            def _(k):
                dproj_copy(m, k, lax.rem(z + n_dp - k, n_dp), z).wait_recv()

        right = dcol[...].reshape(depth, share)
        for i in range(tiles):
            cut = slice(i * (inner_width // tiles), (i + 1) * (inner_width // tiles))
            if depth <= 1024:
                wg_vmem[cut, :] = dot(att_t[cut, :], right)
            else:
                left = att_all[:, :, cut].reshape(depth, inner_width // tiles)
                wg_vmem[cut, :] = dot(left, right, TN)
            keep_grad(i).start()

    def keep_grad(i):
        cut = pl.ds(i * (inner_width // tiles), inner_width // tiles)
        return pltpu.make_async_copy(wg_vmem.at[cut], wg_ref.at[cut], s_g.at[i])

    load_kv.wait()

    @pl.when(jnp.logical_not(first))
    def _():
        for j in range(n_mp * chunks):
            load_wq(j).wait()

    @pl.loop(-1, 2 * groups + 3)
    def _(step):
        def phase(run, m):
            @pl.when(jnp.logical_and(m >= 0, m < groups))
            def _():
                run(m)

        phase(forward_query, step)

        @pl.when(step == jnp.where(first, 0, -1))
        def _():
            load_wo.wait()

        phase(forward_finish, step - held_back - 1)
        phase(forward_share, step - held_back)

        @pl.when(step == jnp.where(first, groups, -1))
        def _():
            turn_weights()

        @pl.when(step == jnp.where(first, groups, 2 * groups + 2))
        def _():
            turn_attended()

        phase(backward_query, step - turn)

        @pl.when(step == jnp.where(first, 2 * groups, 2 * groups + 2))
        def _():
            weight_grad()

        phase(backward_finish, step - turn - 1)
        phase(backward_share, step - turn)

    for i in range(tiles):
        keep_grad(i).wait()

    @pl.loop(0, groups)
    def _(m):
        @pl.loop(1, n_dp)
        def _(k):
            att_copy(m, k, z).wait_send()
            dproj_copy(m, k, z, lax.rem(z + k, n_dp)).wait_send()

        for c in range(chunks):
            for o in range(1, n_mp):
                share_copy(psend, precv, s_p, r_p, m, c, o).wait_send()
                share_copy(bsend, brecv, s_b, r_b, m, c, o).wait_send()

            @pl.when(jnp.logical_not(last))
            def _():
                for o in range(n_mp):
                    forward_copy(m, c, o).wait_send()

            @pl.when(jnp.logical_not(first))
            def _():
                for o in range(n_mp):
                    backward_copy(m, c, o).wait_send()


def result_kernel(out, dx, wg, out_ref, dx_ref, wg_ref, out_v, dx_v, wg_v, in_sems, out_sems):
    parts = in_sems.shape[0] - 2
    size = wg.shape[0] // parts
    cuts = [pl.ds(i * size, size) for i in range(parts)]
    routes = [(wg.at[cut], wg_v.at[cut], wg_ref.at[cut]) for cut in cuts]
    routes += [(out, out_v, out_ref), (dx, dx_v, dx_ref)]
    loads = [
        pltpu.make_async_copy(source, held, in_sems.at[i])
        for i, (source, held, _) in enumerate(routes)
    ]
    stores = [
        pltpu.make_async_copy(held, target, out_sems.at[i])
        for i, (_, held, target) in enumerate(routes)
    ]
    for load in loads:
        load.start()
    for load, store in zip(loads, stores):
        load.wait()
        store.start()
    for store in stores:
        store.wait()


def per_device(latents, caption_kv, caption_mask, query_weight, out_weight, gate, cotangent):
    micro, tok, width = latents.shape[1:]
    n_dp, n_pipe, n_mp = (lax.axis_size("dp"), lax.axis_size("pipe"), lax.axis_size("mp"))
    total_rows = micro * tok
    rows = total_rows // GROUPS
    half = width // n_mp
    chunk = half // CHUNKS
    inner_width = out_weight.shape[1]
    heads = inner_width // HEAD_DIM
    cap = caption_mask.shape[1]
    share = width // n_dp
    bf16, f32 = (jnp.bfloat16, jnp.float32)
    whole = (GROUPS, n_mp, CHUNKS, rows, chunk)
    mine = (GROUPS, CHUNKS, rows, chunk)
    cross = (GROUPS, n_mp - 1, CHUNKS, rows, chunk)
    sem = pltpu.SemaphoreType.DMA
    vmem = pl.BlockSpec(memory_space=pltpu.VMEM)
    tiles = heads // 2 if heads % 2 == 0 and half % (heads // 2 * 128) == 0 else 1
    anywhere = pl.BlockSpec(memory_space=pl.ANY)
    section_out, input_grad, weight_grad = pl.pallas_call(
        functools.partial(relay_kernel, (n_dp, n_pipe, n_mp), tiles),
        out_shape=(
            jax.ShapeDtypeStruct((GROUPS, rows, half), bf16),
            jax.ShapeDtypeStruct((GROUPS, rows, half), bf16),
            jax.ShapeDtypeStruct((inner_width, share), f32),
        ),
        in_specs=[anywhere, anywhere, vmem, anywhere, anywhere, vmem, anywhere],
        out_specs=(vmem, vmem, anywhere),
        scratch_shapes=[
            pltpu.VMEM((n_dp, total_rows, inner_width), bf16),
            pltpu.VMEM((n_dp, total_rows, share), bf16),
            pltpu.VMEM((inner_width, min(n_dp * total_rows, 1024)), bf16),
            pltpu.VMEM((inner_width, share), f32),
            pltpu.VMEM((n_mp * CHUNKS, inner_width, chunk), bf16),
            pltpu.VMEM((n_mp * CHUNKS, chunk, inner_width), bf16),
            pltpu.VMEM(caption_kv.shape[2:], bf16),
            pltpu.VMEM((n_mp * CHUNKS, chunk, inner_width), bf16),
            pltpu.VMEM(out_weight.shape[1:], bf16),
            pltpu.VMEM(whole, bf16),
            pltpu.VMEM(whole, bf16),
            pltpu.VMEM(mine, bf16),
            pltpu.VMEM(mine, bf16),
            pltpu.VMEM(cross, bf16),
            pltpu.VMEM(cross, bf16),
            pltpu.VMEM(cross, bf16),
            pltpu.VMEM(cross, bf16),
            pltpu.VMEM((2,) + mine, f32),
            pltpu.VMEM((GROUPS, heads, rows, cap), f32),
            pltpu.VMEM((GROUPS, rows, inner_width), bf16),
            pltpu.VMEM((GROUPS, rows, 128), f32),
            pltpu.VMEM((GROUPS, rows, inner_width), bf16),
            pltpu.VMEM((GROUPS, rows, 128), f32),
            pltpu.VMEM((n_dp, total_rows, share), bf16),
            sem((2 + n_mp * CHUNKS,)),
            sem((tiles,)),
            sem((GROUPS, CHUNKS, n_mp)),
            sem((GROUPS, n_mp, CHUNKS)),
            sem((GROUPS, CHUNKS, n_mp)),
            sem((GROUPS, n_mp, CHUNKS)),
            sem((GROUPS, n_mp - 1, CHUNKS)),
            sem((GROUPS, n_mp - 1, CHUNKS)),
            sem((GROUPS, n_mp - 1, CHUNKS)),
            sem((GROUPS, n_mp - 1, CHUNKS)),
            sem((GROUPS, n_dp)),
            sem((GROUPS, n_dp)),
            sem((GROUPS, n_dp)),
            sem((GROUPS, n_dp)),
        ],
        compiler_params=pltpu.CompilerParams(
            collective_id=0, has_side_effects=True, vmem_limit_bytes=56 * 2**20
        ),
        name="relay",
    )(
        latents.reshape(GROUPS, rows, width),
        caption_kv[0, 0],
        caption_mask,
        query_weight.reshape(n_mp * CHUNKS, chunk, inner_width),
        out_weight[0],
        gate.reshape(n_mp * CHUNKS, 1, chunk),
        cotangent.reshape(GROUPS, rows, width),
    )
    section_out, input_grad, weight_grad = pl.pallas_call(
        result_kernel,
        out_shape=(
            jax.ShapeDtypeStruct((GROUPS, rows, half), bf16),
            jax.ShapeDtypeStruct((GROUPS, rows, half), bf16),
            jax.ShapeDtypeStruct((inner_width, share), f32),
        ),
        in_specs=[anywhere] * 3,
        out_specs=(anywhere,) * 3,
        scratch_shapes=[
            pltpu.VMEM((GROUPS, rows, half), bf16),
            pltpu.VMEM((GROUPS, rows, half), bf16),
            pltpu.VMEM((inner_width, share), f32),
            sem((tiles + 2,)),
            sem((tiles + 2,)),
        ],
        compiler_params=pltpu.CompilerParams(vmem_limit_bytes=56 * 2**20),
        name="results",
    )(section_out, input_grad, weight_grad)
    shape = (1, 1, micro, tok, half)
    return (section_out.reshape(shape), input_grad.reshape(shape), weight_grad[None])


def solution(mesh):
    return jax.shard_map(
        per_device,
        mesh=mesh,
        in_specs=(
            P("dp", None, None, None),
            P("dp", "pipe", None, None, "mp"),
            P("dp", None),
            P("pipe", None, "mp"),
            P("pipe", "mp", None),
            P("pipe", None),
            P("dp", None, None, None),
        ),
        out_specs=(
            P("pipe", "dp", None, None, "mp"),
            P("pipe", "dp", None, None, "mp"),
            P("pipe", "mp", "dp"),
        ),
        check_vma=False,
    )
```

```python
import functools
import math

import jax
import jax.numpy as jnp
from jax import lax
from jax.experimental import pallas as pl
from jax.experimental.pallas import tpu as pltpu
from jax.sharding import PartitionSpec as P

HEAD_DIM = 128
GROUPS = 2
CHUNKS = 3
MESH = pl.DeviceIdType.MESH
NT = (((1,), (1,)), ((), ()))
TN = (((0,), (0,)), ((), ()))


def dot(a, b, dims=(((1,), (0,)), ((), ()))):
    return lax.dot_general(a, b, dims, preferred_element_type=jnp.float32)


def relay_kernel(
    sizes,
    tiles,
    lat,
    kv_any,
    mask,
    wq_any,
    wo_any,
    gate,
    cot,
    out_ref,
    dx_ref,
    wg_ref,
    att_all,
    dcol,
    att_t,
    wg_vmem,
    wqt,
    wot,
    kv,
    wq,
    wo,
    xbuf,
    dybuf,
    xsend,
    dxsend,
    psend,
    precv,
    bsend,
    brecv,
    own,
    prob_buf,
    qbuf,
    rbuf,
    dqbuf,
    pbuf,
    dpj,
    s_w,
    s_g,
    s_x,
    r_x,
    s_dy,
    r_dy,
    s_p,
    r_p,
    s_b,
    r_b,
    s_att,
    r_att,
    s_dp,
    r_dp,
):
    n_dp, n_pipe, n_mp = sizes
    groups, rows, width = lat.shape
    chunks, chunk = (xbuf.shape[2], xbuf.shape[4])
    inner_width = wo.shape[0]
    heads = inner_width // HEAD_DIM
    share = dpj.shape[2]
    unit = math.gcd(chunk, share)
    per_slab = share // unit
    depth = n_dp * groups * rows
    scale = 1.0 / math.sqrt(HEAD_DIM)
    z = lax.axis_index("dp")
    p = lax.axis_index("pipe")
    y = lax.axis_index("mp")
    first = p == 0
    last = p == n_pipe - 1

    def load(i, src, dst):
        return pltpu.make_async_copy(src, dst, s_w.at[i])

    def load_wq(j):
        return load(2 + j, wq_any.at[j], wq.at[j])

    load_kv = load(0, kv_any, kv)
    load_wo = load(1, wo_any, wo)

    def load_rows(src, dst, sems):
        for m in range(groups):
            for c in range(chunks):
                for h in range(n_mp):
                    begin = (h * chunks + c) * chunk
                    pltpu.make_async_copy(
                        src.at[m, :, pl.ds(begin, chunk)], dst.at[m, h, c], sems.at[m, h, c]
                    ).start()

    @pl.when(first)
    def _():
        load_rows(lat, xbuf, r_x)

    load_kv.start()
    for c in range(chunks):
        for h in range(n_mp):
            load_wq(h * chunks + c).start()
    load_wo.start()

    @pl.when(last)
    def _():
        load_rows(cot, dybuf, r_dy)

    barrier = pltpu.get_barrier_semaphore()

    def greet(target):
        pl.semaphore_signal(barrier, inc=1, device_id=target, device_id_type=MESH)

    for o in range(1, n_mp):
        greet({"mp": lax.rem(y + o, n_mp)})

    @pl.loop(1, n_dp)
    def _(k):
        greet({"dp": lax.rem(z + k, n_dp)})

    @pl.when(jnp.logical_not(first))
    def _():
        for h in range(n_mp):
            greet({"pipe": p - 1, "mp": h})

    @pl.when(jnp.logical_not(last))
    def _():
        for h in range(n_mp):
            greet({"pipe": p + 1, "mp": h})

    edges = first.astype(jnp.int32) + last.astype(jnp.int32)
    pl.semaphore_wait(barrier, (n_mp - 1) + (n_dp - 1) + n_mp * (2 - edges))

    def group_rows(m):
        return pl.ds(pl.multiple_of(m * rows, rows), rows)

    def columns(j):
        return pl.ds(pl.multiple_of(j * chunk, 128), chunk)

    def relay_copy(src, dst, send, recv, m, c, h, target, slot):
        return pltpu.make_async_remote_copy(
            src_ref=src.at[m, c],
            dst_ref=dst.at[m, h, c],
            send_sem=send.at[m, c, slot],
            recv_sem=recv.at[m, h, c],
            device_id=target,
            device_id_type=MESH,
        )

    def forward_copy(m, c, o):
        target = {"pipe": p + 1, "mp": lax.rem(y + o, n_mp)}
        return relay_copy(xsend, xbuf, s_x, r_x, m, c, y, target, o)

    def backward_copy(m, c, o):
        target = {"pipe": p - 1, "mp": lax.rem(y + o, n_mp)}
        return relay_copy(dxsend, dybuf, s_dy, r_dy, m, c, y, target, o)

    def share_copy(src, dst, send, recv, m, c, o):
        return pltpu.make_async_remote_copy(
            src_ref=src.at[m, o - 1, c],
            dst_ref=dst.at[m, o - 1, c],
            send_sem=send.at[m, o - 1, c],
            recv_sem=recv.at[m, o - 1, c],
            device_id={"mp": lax.rem(y + o, n_mp)},
            device_id_type=MESH,
        )

    def att_copy(m, k, source):
        piece = att_all.at[source, group_rows(m)]
        return pltpu.make_async_remote_copy(
            src_ref=piece,
            dst_ref=piece,
            send_sem=s_att.at[m, k],
            recv_sem=r_att.at[m, k],
            device_id={"dp": lax.rem(z + k, n_dp)},
            device_id_type=MESH,
        )

    def dproj_copy(m, k, source, owner):
        return pltpu.make_async_remote_copy(
            src_ref=dpj.at[owner, group_rows(m)],
            dst_ref=dcol.at[source, group_rows(m)],
            send_sem=s_dp.at[m, k],
            recv_sem=r_dp.at[m, k],
            device_id={"dp": lax.rem(z + k, n_dp)},
            device_id_type=MESH,
        )

    def head(t):
        return slice(t * HEAD_DIM, (t + 1) * HEAD_DIM)

    def fold(values):
        pieces = [values[:, i : i + 128] for i in range(0, values.shape[1], 128)]
        return functools.reduce(jnp.add, pieces)

    order = [(c, o) for c in range(chunks) for o in range(n_mp)]

    def forward_query(m):
        query_raw = jnp.zeros((rows, inner_width), jnp.float32)
        squares = jnp.zeros((rows, 128), jnp.float32)
        for c, o in order:
            h = lax.rem(y + o, n_mp)
            if o == 0:
                for g in range(n_mp):
                    relay_copy(xsend, xbuf, s_x, r_x, m, c, g, {"mp": y}, 0).wait_recv()

                @pl.when(jnp.logical_and(first, m == 0))
                def _():
                    for g in range(n_mp):
                        load_wq(g * chunks + c).wait()

            x = xbuf[m, h, c]
            query_raw += dot(x, wq[h * chunks + c])
            squares += fold(jnp.square(x.astype(jnp.float32)))
        squares = jnp.sum(squares, axis=-1, keepdims=True)
        scale_r = lax.rsqrt(squares / width + 1e-06)
        query = (query_raw * scale_r).astype(jnp.bfloat16)
        rbuf[m] = jnp.broadcast_to(scale_r, rbuf.shape[1:])
        qbuf[m] = query
        live = mask[...] > 0
        scores = jnp.stack([dot(query[:, head(t)], kv[0, :, head(t)], NT) for t in range(heads)])
        scores = jnp.where(live[None], scores * scale, -1e30)
        powers = jnp.exp(scores - jnp.max(scores, axis=-1, keepdims=True))
        prob = powers * (1.0 / jnp.sum(powers, axis=-1, keepdims=True))
        prob_buf[m] = prob
        probs = prob.astype(jnp.bfloat16)
        parts = [dot(probs[t], kv[1, :, head(t)]).astype(jnp.bfloat16) for t in range(heads)]
        att_all[z, group_rows(m)] = jnp.concatenate(parts, axis=1)

    def forward_share(m):
        attended = att_all[z, group_rows(m)]
        for o in range(1, n_mp):
            h = lax.rem(y + o, n_mp)
            for c in range(chunks):
                piece = dot(attended, wo[:, columns(h * chunks + c)])
                psend[m, o - 1, c] = piece.astype(jnp.bfloat16)
                share_copy(psend, precv, s_p, r_p, m, c, o).start()
        for c in range(chunks):
            own[0, m, c] = dot(attended, wo[:, columns(y * chunks + c)])

        @pl.loop(1, n_dp)
        def _(k):
            att_copy(m, k, z).start()

    def forward_finish(m):
        for c in range(chunks):
            total = own[0, m, c]
            for o in range(1, n_mp):
                share_copy(psend, precv, s_p, r_p, m, c, o).wait_recv()
                total += precv[m, o - 1, c].astype(jnp.float32)
            x_float = xbuf[m, y, c].astype(jnp.float32)
            result = (x_float + gate[y * chunks + c] * total).astype(jnp.bfloat16)
            xsend[m, c] = result

            @pl.when(jnp.logical_not(last))
            def _():
                for o in reversed(range(n_mp)):
                    forward_copy(m, c, o).start()

            out_ref[m, :, c * chunk : (c + 1) * chunk] = result

    def backward_query(m):
        d_att = jnp.zeros((rows, inner_width), jnp.float32)
        for c, o in order:
            h = lax.rem(y + o, n_mp)
            j = h * chunks + c

            if o == 0:
                for g in range(n_mp):
                    relay_copy(dxsend, dybuf, s_dy, r_dy, m, c, g, {"mp": y}, 0).wait_recv()

            dproj = (gate[j] * dybuf[m, h, c].astype(jnp.float32)).astype(jnp.bfloat16)
            for t in range(chunk // unit):
                index = j * (chunk // unit) + t
                piece = dproj[:, t * unit : (t + 1) * unit]
                if per_slab == 1:
                    dpj[index, group_rows(m)] = piece
                else:
                    begin = pl.multiple_of(lax.rem(index, per_slab) * unit, unit)
                    dpj[lax.div(index, per_slab), group_rows(m), pl.ds(begin, unit)] = piece
            d_att += dot(dproj, wot[j])

        @pl.loop(1, n_dp)
        def _(k):
            dproj_copy(m, k, z, lax.rem(z + k, n_dp)).start()

        d_att = d_att.astype(jnp.bfloat16)
        prob = prob_buf[m]
        d_prob = jnp.stack([dot(d_att[:, head(t)], kv[1, :, head(t)], NT) for t in range(heads)])
        mean = jnp.sum(prob * d_prob, axis=-1, keepdims=True)
        d_score = (prob * (d_prob - mean)).astype(jnp.bfloat16)
        parts = [dot(d_score[t], kv[0, :, head(t)]) for t in range(heads)]
        d_query = (jnp.concatenate(parts, axis=1) * scale).astype(jnp.bfloat16)
        dqbuf[m] = d_query
        both = d_query.astype(jnp.float32) * qbuf[m].astype(jnp.float32)
        inner = jnp.sum(fold(both), axis=-1, keepdims=True)
        pbuf[m] = jnp.broadcast_to(rbuf[m][:, :1] * inner / width, pbuf.shape[1:])

    def backward_share(m):
        d_query = dqbuf[m]
        pull = pbuf[m][:, :1]

        def piece_of(h, c):
            x_float = xbuf[m, h, c].astype(jnp.float32)
            return dot(d_query, wqt[h * chunks + c]) - x_float * pull

        for o in range(1, n_mp):
            h = lax.rem(y + o, n_mp)
            for c in range(chunks):
                bsend[m, o - 1, c] = piece_of(h, c).astype(jnp.bfloat16)
                share_copy(bsend, brecv, s_b, r_b, m, c, o).start()
        for c in range(chunks):
            own[1, m, c] = piece_of(y, c)

    def backward_finish(m):
        scale_r = rbuf[m][:, :1]
        for c in range(chunks):
            total = own[1, m, c]
            for o in range(1, n_mp):
                share_copy(bsend, brecv, s_b, r_b, m, c, o).wait_recv()
                total += brecv[m, o - 1, c].astype(jnp.float32)
            dy = dybuf[m, y, c].astype(jnp.float32)
            result = (dy + scale_r * total).astype(jnp.bfloat16)
            dxsend[m, c] = result

            @pl.when(jnp.logical_not(first))
            def _():
                for o in reversed(range(n_mp)):
                    backward_copy(m, c, o).start()

            dx_ref[m, :, c * chunk : (c + 1) * chunk] = result

    late = last.astype(jnp.int32)
    turn = groups * (1 - late)
    held_back = (groups + 1) * late

    def turn_weights():
        @pl.loop(0, n_mp * chunks)
        def _(j):
            wqt[j] = wq[j].T
            wot[j] = wo[:, columns(j)].T

    def turn_attended():
        @pl.loop(0, groups)
        def _(m):
            @pl.loop(1, n_dp)
            def _(k):
                att_copy(m, k, lax.rem(z + n_dp - k, n_dp)).wait_recv()

        if depth <= 1024:
            att_t[...] = att_all[...].reshape(depth, inner_width).T

    def weight_grad():
        dcol[z] = dpj[z]

        @pl.loop(0, groups)
        def _(m):
            @pl.loop(1, n_dp)
            def _(k):
                dproj_copy(m, k, lax.rem(z + n_dp - k, n_dp), z).wait_recv()

        right = dcol[...].reshape(depth, share)
        for i in range(tiles):
            cut = slice(i * (inner_width // tiles), (i + 1) * (inner_width // tiles))
            if depth <= 1024:
                wg_vmem[cut, :] = dot(att_t[cut, :], right)
            else:
                left = att_all[:, :, cut].reshape(depth, inner_width // tiles)
                wg_vmem[cut, :] = dot(left, right, TN)
            keep_grad(i).start()

    def keep_grad(i):
        cut = pl.ds(i * (inner_width // tiles), inner_width // tiles)
        return pltpu.make_async_copy(wg_vmem.at[cut], wg_ref.at[cut], s_g.at[i])

    load_kv.wait()

    @pl.when(jnp.logical_not(first))
    def _():
        for j in range(n_mp * chunks):
            load_wq(j).wait()

    @pl.loop(-1, 2 * groups + 3)
    def _(step):
        def phase(run, m):
            @pl.when(jnp.logical_and(m >= 0, m < groups))
            def _():
                run(m)

        phase(forward_query, step)

        @pl.when(step == jnp.where(first, 0, -1))
        def _():
            load_wo.wait()

        phase(forward_finish, step - held_back - 1)
        phase(forward_share, step - held_back)

        @pl.when(step == jnp.where(first, groups, -1))
        def _():
            turn_weights()

        @pl.when(step == jnp.where(first, groups, 2 * groups + 2))
        def _():
            turn_attended()

        phase(backward_query, step - turn)

        @pl.when(step == jnp.where(first, 2 * groups, 2 * groups + 2))
        def _():
            weight_grad()

        phase(backward_finish, step - turn - 1)
        phase(backward_share, step - turn)

    for i in range(tiles):
        keep_grad(i).wait()

    @pl.loop(0, groups)
    def _(m):
        @pl.loop(1, n_dp)
        def _(k):
            att_copy(m, k, z).wait_send()
            dproj_copy(m, k, z, lax.rem(z + k, n_dp)).wait_send()

        for c in range(chunks):
            for o in range(1, n_mp):
                share_copy(psend, precv, s_p, r_p, m, c, o).wait_send()
                share_copy(bsend, brecv, s_b, r_b, m, c, o).wait_send()

            @pl.when(jnp.logical_not(last))
            def _():
                for o in range(n_mp):
                    forward_copy(m, c, o).wait_send()

            @pl.when(jnp.logical_not(first))
            def _():
                for o in range(n_mp):
                    backward_copy(m, c, o).wait_send()


def result_kernel(out, dx, wg, out_ref, dx_ref, wg_ref, out_v, dx_v, wg_v, in_sems, out_sems):
    parts = in_sems.shape[0] - 2
    size = wg.shape[0] // parts
    cuts = [pl.ds(i * size, size) for i in range(parts)]
    routes = [(wg.at[cut], wg_v.at[cut], wg_ref.at[cut]) for cut in cuts]
    routes += [(out, out_v, out_ref), (dx, dx_v, dx_ref)]
    loads = [
        pltpu.make_async_copy(source, held, in_sems.at[i])
        for i, (source, held, _) in enumerate(routes)
    ]
    stores = [
        pltpu.make_async_copy(held, target, out_sems.at[i])
        for i, (_, held, target) in enumerate(routes)
    ]
    for load in loads:
        load.start()
    for load, store in zip(loads, stores):
        load.wait()
        store.start()
    for store in stores:
        store.wait()


def per_device(latents, caption_kv, caption_mask, query_weight, out_weight, gate, cotangent):
    micro, tok, width = latents.shape[1:]
    n_dp, n_pipe, n_mp = (lax.axis_size("dp"), lax.axis_size("pipe"), lax.axis_size("mp"))
    total_rows = micro * tok
    rows = total_rows // GROUPS
    half = width // n_mp
    chunk = half // CHUNKS
    inner_width = out_weight.shape[1]
    heads = inner_width // HEAD_DIM
    cap = caption_mask.shape[1]
    share = width // n_dp
    bf16, f32 = (jnp.bfloat16, jnp.float32)
    whole = (GROUPS, n_mp, CHUNKS, rows, chunk)
    mine = (GROUPS, CHUNKS, rows, chunk)
    cross = (GROUPS, n_mp - 1, CHUNKS, rows, chunk)
    sem = pltpu.SemaphoreType.DMA
    vmem = pl.BlockSpec(memory_space=pltpu.VMEM)
    tiles = heads // 2 if heads % 2 == 0 and half % (heads // 2 * 128) == 0 else 1
    anywhere = pl.BlockSpec(memory_space=pl.ANY)
    section_out, input_grad, weight_grad = pl.pallas_call(
        functools.partial(relay_kernel, (n_dp, n_pipe, n_mp), tiles),
        out_shape=(
            jax.ShapeDtypeStruct((GROUPS, rows, half), bf16),
            jax.ShapeDtypeStruct((GROUPS, rows, half), bf16),
            jax.ShapeDtypeStruct((inner_width, share), f32),
        ),
        in_specs=[anywhere, anywhere, vmem, anywhere, anywhere, vmem, anywhere],
        out_specs=(vmem, vmem, anywhere),
        scratch_shapes=[
            pltpu.VMEM((n_dp, total_rows, inner_width), bf16),
            pltpu.VMEM((n_dp, total_rows, share), bf16),
            pltpu.VMEM((inner_width, min(n_dp * total_rows, 1024)), bf16),
            pltpu.VMEM((inner_width, share), f32),
            pltpu.VMEM((n_mp * CHUNKS, inner_width, chunk), bf16),
            pltpu.VMEM((n_mp * CHUNKS, chunk, inner_width), bf16),
            pltpu.VMEM(caption_kv.shape[2:], bf16),
            pltpu.VMEM((n_mp * CHUNKS, chunk, inner_width), bf16),
            pltpu.VMEM(out_weight.shape[1:], bf16),
            pltpu.VMEM(whole, bf16),
            pltpu.VMEM(whole, bf16),
            pltpu.VMEM(mine, bf16),
            pltpu.VMEM(mine, bf16),
            pltpu.VMEM(cross, bf16),
            pltpu.VMEM(cross, bf16),
            pltpu.VMEM(cross, bf16),
            pltpu.VMEM(cross, bf16),
            pltpu.VMEM((2,) + mine, f32),
            pltpu.VMEM((GROUPS, heads, rows, cap), f32),
            pltpu.VMEM((GROUPS, rows, inner_width), bf16),
            pltpu.VMEM((GROUPS, rows, 128), f32),
            pltpu.VMEM((GROUPS, rows, inner_width), bf16),
            pltpu.VMEM((GROUPS, rows, 128), f32),
            pltpu.VMEM((n_dp, total_rows, share), bf16),
            sem((2 + n_mp * CHUNKS,)),
            sem((tiles,)),
            sem((GROUPS, CHUNKS, n_mp)),
            sem((GROUPS, n_mp, CHUNKS)),
            sem((GROUPS, CHUNKS, n_mp)),
            sem((GROUPS, n_mp, CHUNKS)),
            sem((GROUPS, n_mp - 1, CHUNKS)),
            sem((GROUPS, n_mp - 1, CHUNKS)),
            sem((GROUPS, n_mp - 1, CHUNKS)),
            sem((GROUPS, n_mp - 1, CHUNKS)),
            sem((GROUPS, n_dp)),
            sem((GROUPS, n_dp)),
            sem((GROUPS, n_dp)),
            sem((GROUPS, n_dp)),
        ],
        compiler_params=pltpu.CompilerParams(
            collective_id=0, has_side_effects=True, vmem_limit_bytes=56 * 2**20
        ),
        name="relay",
    )(
        latents.reshape(GROUPS, rows, width),
        caption_kv[0, 0],
        caption_mask,
        query_weight.reshape(n_mp * CHUNKS, chunk, inner_width),
        out_weight[0],
        gate.reshape(n_mp * CHUNKS, 1, chunk),
        cotangent.reshape(GROUPS, rows, width),
    )
    section_out, input_grad, weight_grad = pl.pallas_call(
        result_kernel,
        out_shape=(
            jax.ShapeDtypeStruct((GROUPS, rows, half), bf16),
            jax.ShapeDtypeStruct((GROUPS, rows, half), bf16),
            jax.ShapeDtypeStruct((inner_width, share), f32),
        ),
        in_specs=[anywhere] * 3,
        out_specs=(anywhere,) * 3,
        scratch_shapes=[
            pltpu.VMEM((GROUPS, rows, half), bf16),
            pltpu.VMEM((GROUPS, rows, half), bf16),
            pltpu.VMEM((inner_width, share), f32),
            sem((tiles + 2,)),
            sem((tiles + 2,)),
        ],
        compiler_params=pltpu.CompilerParams(vmem_limit_bytes=56 * 2**20),
        name="results",
    )(section_out, input_grad, weight_grad)
    shape = (1, 1, micro, tok, half)
    return (section_out.reshape(shape), input_grad.reshape(shape), weight_grad[None])


def solution(mesh):
    return jax.shard_map(
        per_device,
        mesh=mesh,
        in_specs=(
            P("dp", None, None, None),
            P("dp", "pipe", None, None, "mp"),
            P("dp", None),
            P("pipe", None, "mp"),
            P("pipe", "mp", None),
            P("pipe", None),
            P("dp", None, None, None),
        ),
        out_specs=(
            P("pipe", "dp", None, None, "mp"),
            P("pipe", "dp", None, None, "mp"),
            P("pipe", "mp", "dp"),
        ),
        check_vma=False,
    )
```
